512 devices in a mesh: rep: 64 (over y, z), tp: 8 (over x, core).
Axes of the slice: x: 4, y: 8, z: 8, core: 2. Of those that a mesh axis runs over, the one named last changes fastest.
Arguments:
- queries: bfloat16 [2048, 4, 8192], P('rep', None, 'tp'), may hold values from -400 to 400
- new_keys: bfloat16 [2048, 4, 1024], P('rep', None, 'tp'), may hold values from -8 to 8
- new_values: bfloat16 [2048, 4, 1024], P('rep', None, 'tp'), may hold values from -6 to 6
- key_pool: bfloat16 [8192, 64, 1024], P('rep', None, 'tp'), may hold values from -6 to 6
- value_pool: bfloat16 [8192, 64, 1024], P('rep', None, 'tp'), may hold values from -400 to 400
- block_table: int32 [2048, 2], P('rep'), may hold values from 0 to 127, as said below
- context: int32 [2048], P('rep'), may hold values from 1 to 128
- move_source: int32 [4096], P('rep'), may hold values from 0 to 127
- move_replica: int32 [4096], P('rep'), may hold values from 0 to 63, as said below
- move_target: int32 [4096], P('rep'), may hold values from 0 to 127, as said below
- norm_gain: float32 [8192], P('tp'), may hold values from 0.1 to 1.9
Outputs:
- normed: float32 [2048, 4, 8192], P('rep', None, 'tp')
The draws below stay inside these ranges and needn't reach their ends.
Inputs may be any that keep to these rules, and one draw needn't show every extreme that they name: `block_table`: the 2 slots of the requests of one replica are distinct; no such slot is the move_source of an entry of that replica. An entry whose move_replica is its own replica has move_target equal to move_source. Any other entry moves its page to another replica; at most 2 such entries of one replica name the same receiving replica, and some replica sends exactly 2 to some other; one replica receives at most 64 pages, and some replica receives exactly 64. `move_target`: the targets of pages moved into one replica are distinct slots of that replica's block tables.
All inputs are finite; a program needn't handle non-finite values.
Results may differ from the reference program's by a relative error of at most 0.0022.
Values may be sent and summed in bfloat16 or wider, within the bound.
A program may use at most 64 MiB of HBM per device.

```python
import math
import jax
import jax.numpy as jnp
from jax import lax

QH = 64
KVH = 8
HD = 128
PAGE = 64
MAXP = 2
STEPS = 4
CAP = 2
REQ = 32
OUT = 64
PAGES = 128
ROWS = 2048
ALLPAGES = 8192
MOVES = 4096
N_REP = 64


def migration_plan(key):
    subkeys = jax.random.split(key, 8)
    orders = jax.vmap(lambda item: jax.random.permutation(item, PAGES))(jax.random.split(subkeys[0], N_REP)).astype(jnp.int32)
    tables = orders[:, :REQ * MAXP].reshape(N_REP, REQ, MAXP)
    spares = orders[:, REQ * MAXP:]
    circle_order = jax.random.permutation(subkeys[1], N_REP).astype(jnp.int32)
    positions = jnp.argsort(circle_order).astype(jnp.int32)
    send_counts = jax.random.randint(subkeys[2], (N_REP,), OUT * 3 // 4, OUT + 1)
    filled = jax.random.randint(subkeys[3], (), 0, N_REP)
    behind = (filled - positions) % N_REP
    send_counts = jnp.where((behind >= 1) & (behind <= OUT // CAP), OUT, send_counts)
    takers = jax.vmap(lambda item: jax.random.permutation(item, REQ))(jax.random.split(subkeys[4], N_REP)).astype(jnp.int32)
    taker_rank = jnp.argsort(takers, axis=1)
    receiving = taker_rank < OUT // MAXP
    lengths = jax.random.randint(subkeys[5], (N_REP, REQ), 1, MAXP * PAGE + 1)
    lengths = jnp.where(receiving, jnp.maximum(lengths, (MAXP - 1) * PAGE + 1), lengths).reshape(ROWS)
    longest = jax.random.randint(subkeys[6], (), 0, ROWS)
    lengths = lengths.at[longest].set(MAXP * PAGE).astype(jnp.int32)
    entry_ids = jnp.arange(OUT, dtype=jnp.int32)[None, :]
    sources = jnp.arange(N_REP, dtype=jnp.int32)[:, None]
    receivers = circle_order[(positions[:, None] + 1 + entry_ids // CAP) % N_REP]
    requests = takers[receivers, entry_ids // MAXP]
    landing = tables[receivers, requests, entry_ids % MAXP]
    valid = entry_ids < send_counts[:, None]
    replicas_out = jnp.where(valid, receivers, sources)
    targets_out = jnp.where(valid, landing, spares)
    shuffles = jax.vmap(lambda item: jax.random.permutation(item, OUT))(jax.random.split(subkeys[7], N_REP)).astype(jnp.int32)
    slots_out = jnp.take_along_axis(spares, shuffles, axis=1)
    replicas_out = jnp.take_along_axis(replicas_out, shuffles, axis=1)
    targets_out = jnp.take_along_axis(targets_out, shuffles, axis=1)
    return (tables.reshape(ROWS, MAXP).astype(jnp.int32), lengths, slots_out.reshape(MOVES).astype(jnp.int32), replicas_out.reshape(MOVES).astype(jnp.int32), targets_out.reshape(MOVES).astype(jnp.int32))


def drawn_parts(key):
    subkeys = jax.random.split(jax.random.fold_in(key, 500), 1)
    base_rows = jnp.clip(jax.random.normal(subkeys[0], (ROWS, KVH * HD), jnp.float32), -6.0, 6.0)
    return base_rows


def draw_block_table(key, part):
    return migration_plan(key)[0]


def draw_context(key, part):
    return migration_plan(key)[1]


def draw_move_source(key, part):
    return migration_plan(key)[2]


def draw_move_replica(key, part):
    return migration_plan(key)[3]


def draw_move_target(key, part):
    return migration_plan(key)[4]


def draw_queries(key, part):
    key = jax.random.fold_in(key, 1)
    subkeys = jax.random.split(key, 1)
    return jnp.clip(jax.random.normal(subkeys[0], (ROWS, STEPS, QH * HD), jnp.float32), -6.0, 6.0).astype(jnp.bfloat16)


def draw_new_keys(key, part):
    base_rows = drawn_parts(key)
    key = jax.random.fold_in(key, 2)
    drawn = jnp.clip(jax.random.normal(key, (ROWS, STEPS, KVH * HD), jnp.float32), -6.0, 6.0)
    return drawn.at[:, 0, :].set(base_rows).astype(jnp.bfloat16)


def draw_value_pool(key, part):
    key = jax.random.fold_in(key, 3)
    subkeys = jax.random.split(key, 3)
    page_scale = jnp.exp(jax.random.uniform(subkeys[1], (ALLPAGES, 1, 1), minval=jnp.log(0.5), maxval=jnp.log(5.0)))
    column_scale = jnp.exp(jax.random.uniform(subkeys[2], (1, 1, KVH * HD), minval=jnp.log(0.4), maxval=jnp.log(4.0)))
    head_place = (jnp.arange(KVH * HD) // HD).astype(jnp.float32) / max(KVH - 1, 1)
    rising = (3.0 ** head_place)[None, None, :]
    drawn = jnp.clip(jax.random.normal(subkeys[0], (ALLPAGES, PAGE, KVH * HD), jnp.float32), -6.0, 6.0)
    return (drawn * page_scale * column_scale * rising).astype(jnp.bfloat16)


def block_levels(key, extent, pieces, smallest, top_value):
    def one(position, blocks):
        draws = jax.random.uniform(jax.random.fold_in(jax.random.fold_in(key, 6), position), (blocks,), jnp.float32, smallest / len(pieces), top_value / len(pieces))
        return jnp.repeat(jnp.exp(draws), extent[position] // blocks).reshape((-1,) + (1,) * (len(extent) - position - 1))

    level = one(*pieces[0])
    for cut in pieces[1:]:
        level = level * one(*cut)
    return level


def noise(stream_key, extent, spread, most, shards=(), held_as=jnp.bfloat16):
    values = jax.random.normal(stream_key, extent, jnp.float32) * spread
    if len(shards) > 0:
        values = block_levels(stream_key, extent, shards, -0.22, 0.18) * values
    return jnp.clip(values, min=-most, max=most).astype(held_as)


def setup_inputs(seed: int = 0) -> dict:
    seeds = jax.random.split(jax.random.key(seed), 12)
    return {
        "queries": draw_queries(jax.random.fold_in(seeds[11], 71), 0),
        "new_keys": draw_new_keys(jax.random.fold_in(seeds[11], 71), 0),
        "new_values": noise(seeds[2], (ROWS, STEPS, KVH * HD), 1.0, 6.0, ((0, 64), (2, 8))),
        "key_pool": noise(seeds[3], (ALLPAGES, PAGE, KVH * HD), 1.0, 6.0, ((0, 64), (2, 8))),
        "value_pool": draw_value_pool(jax.random.fold_in(seeds[11], 71), 0),
        "block_table": draw_block_table(jax.random.fold_in(seeds[11], 71), 0),
        "context": draw_context(jax.random.fold_in(seeds[11], 71), 0),
        "move_source": draw_move_source(jax.random.fold_in(seeds[11], 71), 0),
        "move_replica": draw_move_replica(jax.random.fold_in(seeds[11], 71), 0),
        "move_target": draw_move_target(jax.random.fold_in(seeds[11], 71), 0),
        "norm_gain": jnp.clip(1.0 + 0.18 * jax.random.normal(seeds[10], (QH * HD,), jnp.float32), 0.1, 1.9),
    }


MASKED = -1e+30

def partials(grouped, key_blocks, value_blocks, allowed):
    scaling = 1.0 / math.sqrt(HD)
    scores = jnp.einsum('rtkgd,rpjkd->rptkgj', grouped.astype(jnp.float32), key_blocks.astype(jnp.float32)) * scaling
    scores = jnp.where(allowed[:, :, :, None, None, :], scores, MASKED)
    maxima = lax.optimization_barrier(jnp.max(scores, axis=-1))
    weights = jnp.exp(scores - maxima[..., None])
    totals = lax.optimization_barrier(jnp.sum(weights, axis=-1))
    rounded = weights.astype(jnp.bfloat16).astype(jnp.float32)
    accumulated = jnp.einsum('rptkgj,rpjkd->rptkgd', rounded, value_blocks.astype(jnp.float32))
    return (maxima, totals, accumulated)

def combine(maxima, totals, accumulated):
    largest = lax.optimization_barrier(jnp.max(maxima, axis=1))
    factors = jnp.exp(maxima - largest[:, None])
    numerator = lax.optimization_barrier(jnp.sum(factors[..., None] * accumulated, axis=1))
    denominator = lax.optimization_barrier(jnp.sum(factors * totals, axis=1))
    return numerator / denominator[..., None]

def reference(queries, new_keys, new_values, key_pool, value_pool, block_table, context, move_source, move_replica, move_target, norm_gain):
    group = QH // KVH
    anchor = (jnp.arange(MOVES, dtype=jnp.int32) // OUT).astype(jnp.int32)
    source_rows = (anchor * PAGES + move_source).astype(jnp.int32)
    positions = jnp.arange(MAXP, dtype=jnp.int32)[:, None] * PAGE + jnp.arange(PAGE, dtype=jnp.int32)[None, :]
    causal = jnp.arange(STEPS, dtype=jnp.int32)[None, :] <= jnp.arange(STEPS, dtype=jnp.int32)[:, None]

    def replica(index):
        moving = (move_replica == index) & (anchor != index)
        order = jnp.argsort(jnp.where(moving, 0, 1).astype(jnp.int32), stable=True)[:OUT].astype(jnp.int32)
        targets = jnp.where(moving[order], move_target[order], PAGES).astype(jnp.int32)
        start = (index * PAGES).astype(jnp.int32)
        keys_here = lax.dynamic_slice_in_dim(key_pool, start, PAGES, 0).at[targets].set(key_pool[source_rows[order]], mode='drop')
        values_here = lax.dynamic_slice_in_dim(value_pool, start, PAGES, 0).at[targets].set(value_pool[source_rows[order]], mode='drop')
        row_start = (index * REQ).astype(jnp.int32)
        grouped = lax.dynamic_slice_in_dim(queries, row_start, REQ, 0).reshape(REQ, STEPS, KVH, group, HD)
        table = lax.dynamic_slice_in_dim(block_table, row_start, REQ, 0)
        lengths = lax.dynamic_slice_in_dim(context, row_start, REQ, 0)
        cache_keys = keys_here[table].reshape(REQ, MAXP, PAGE, KVH, HD)
        cache_values = values_here[table].reshape(REQ, MAXP, PAGE, KVH, HD)
        live_mask = positions[None] < lengths[:, None, None]
        cache_allowed = jnp.broadcast_to(live_mask[:, :, None, :], (REQ, MAXP, STEPS, PAGE))
        first = partials(grouped, cache_keys, cache_values, cache_allowed)
        draft_keys = lax.dynamic_slice_in_dim(new_keys, row_start, REQ, 0).reshape(REQ, 1, STEPS, KVH, HD)
        draft_values = lax.dynamic_slice_in_dim(new_values, row_start, REQ, 0).reshape(REQ, 1, STEPS, KVH, HD)
        draft_allowed = jnp.broadcast_to(causal[None, None], (REQ, 1, STEPS, STEPS))
        second = partials(grouped, draft_keys, draft_values, draft_allowed)
        attention = combine(jnp.concatenate([first[0], second[0]], axis=1), jnp.concatenate([first[1], second[1]], axis=1), jnp.concatenate([first[2], second[2]], axis=1)).reshape(REQ, STEPS, QH * HD)
        mean_square = lax.optimization_barrier(jnp.sum(attention * attention, axis=-1)) / (QH * HD)
        return attention * lax.rsqrt(mean_square + 1e-05)[..., None] * norm_gain
    result = lax.map(replica, jnp.arange(N_REP, dtype=jnp.int32))
    return result.reshape(ROWS, STEPS, QH * HD)
```

```python
import functools
import math

import jax
import jax.numpy as jnp
from jax import lax
from jax.experimental import pallas as pl
from jax.experimental.pallas import tpu as pltpu
from jax.sharding import PartitionSpec as P

HD = 128
MASKED = -1e30
HUGE = 3e38
TOP = 32767.0
MESH = pl.DeviceIdType.MESH
I32 = jnp.int32
F32 = jnp.float32
BF16 = jnp.bfloat16


def iota(shape, dim):
    return lax.broadcasted_iota(I32, shape, dim)


def to_column(row, size):
    shape = (size, size)
    return jnp.sum(jnp.where(iota(shape, 0) == iota(shape, 1), row, 0.0), axis=1, keepdims=True)


def to_row(column, size):
    shape = (size, size)
    return jnp.sum(jnp.where(iota(shape, 0) == iota(shape, 1), column, 0.0), axis=0, keepdims=True)


def block_sums(queries, keys, values, caps):
    scores = lax.dot_general(queries, keys, (((1,), (1,)), ((), ())), preferred_element_type=F32)
    scores = jnp.minimum(scores * (1.0 / math.sqrt(HD)), caps)
    maxima = jnp.max(scores, axis=1, keepdims=True)
    weights = jnp.exp(scores - maxima)
    totals = jnp.sum(weights, axis=1, keepdims=True)
    sums = jnp.dot(weights.astype(BF16), values, preferred_element_type=F32)
    return maxima, totals, sums


def kernel(
    n, nz, tp,
    table_s, context_s,
    q_ref, nk_ref, nv_ref, kp_ref, vp_ref, table_ref, context_ref, source_ref, replica_ref, target_ref, gain_ref,
    out_ref,
    kv, vv, qf, qb, nk, nv,
    note_out, note_in, lists, lists_s, caps,
    q_out, q_in, sum_out, sum_in, stat_out, stat_in,
    near, near_log, draft, draft_log, attention, squares, scales, norm_rows,
    pool_sem, list_sem, note_send, note_recv, q_send, q_recv, sum_send, sum_recv, stat_send, stat_recv, norm_send, norm_recv,
):
    ny = n // nz
    requests, steps, width = q_ref.shape
    heads = width // HD
    rows = steps * heads
    entries = replica_ref.shape[1]
    slots = kp_ref.shape[0]
    page = kp_ref.shape[1]
    me = lax.axis_index("rep")
    lane_me = lax.axis_index("tp")
    my, mz = lax.div(me, nz), lax.rem(me, nz)

    def ahead(q):
        return lax.rem(my + lax.div(q, nz), ny) * nz + lax.rem(mz + lax.rem(q, nz), nz)

    def behind(q):
        return lax.rem(my + ny - lax.div(q, nz), ny) * nz + lax.rem(mz + nz - lax.rem(q, nz), nz)

    def opposite(q):
        return lax.rem(ny - lax.div(q, nz), ny) * nz + lax.rem(nz - lax.rem(q, nz), nz)

    def order(step):
        return lax.rem((step + 1) * 27, n)

    barrier = pltpu.get_barrier_semaphore()

    def greet(step, carry):
        pl.semaphore_signal(barrier, inc=1, device_id=(ahead(step + 1), lane_me), device_id_type=MESH)
        return carry

    lax.fori_loop(0, n - 1, greet, 0)
    for other in range(1, tp):
        pl.semaphore_signal(barrier, inc=1, device_id=(me, lax.rem(lane_me + other, tp)), device_id_type=MESH)

    pool_copies = [
        pltpu.make_async_copy(kp_ref, kv, pool_sem.at[0]),
        pltpu.make_async_copy(vp_ref, vv, pool_sem.at[1]),
    ]
    for copy in pool_copies:
        copy.start()

    replica = replica_ref[...].astype(F32)
    source = source_ref[...].astype(F32)
    target = target_ref[...].astype(F32)
    square = (entries, entries)
    replica_c = to_column(replica, entries)
    same_before = (replica_c == replica) & (iota(square, 0) < iota(square, 1))
    rank = jnp.sum(jnp.where(same_before, 1.0, 0.0), axis=0, keepdims=True)
    rank_c = to_column(rank, entries)
    source_c = to_column(source, entries)

    def vector_peer(q, sign):
        dy, dz = q // nz, q % nz
        return (((my + ny + sign * dy) % ny) * nz + (mz + nz + sign * dz) % nz).astype(F32)

    def targets_of(sign):
        peers = vector_peer(iota((n, entries), 0), sign)
        found = []
        for k in range(2):
            chosen = (peers == replica) & (rank == float(k))
            found.append(jnp.sum(jnp.where(chosen, target + 1.0, 0.0), axis=1, keepdims=True) - 1.0)
        return found

    wide = (entries, 2 * n)
    peers_row = vector_peer(iota(wide, 1) % n, 1)
    chosen = (replica_c == peers_row) & (rank_c == (iota(wide, 1) // n).astype(F32))
    source_row = jnp.sum(jnp.where(chosen, source_c, 0.0), axis=0, keepdims=True)

    context_c = to_column(context_ref[...].astype(F32), requests)
    by_slot = (requests, slots)
    slot_lane = iota(by_slot, 1).astype(F32)
    request_c = iota(by_slot, 0).astype(F32)
    valid_row = jnp.zeros((1, slots), F32)
    place_row = jnp.zeros((1, slots), F32)
    for p in range(2):
        table_c = to_column(table_ref[p : p + 1, :].astype(F32), requests)
        here = table_c == slot_lane
        valid = jnp.clip(context_c - float(p * page), 0.0, float(page))
        valid_row += jnp.sum(jnp.where(here, valid, 0.0), axis=0, keepdims=True)
        place_row += jnp.sum(jnp.where(here, request_c + float(p * requests), 0.0), axis=0, keepdims=True)

    notes = (n, slots)
    lane = iota(notes, 1).astype(F32)
    first, second = targets_of(1)
    marks = jnp.where(lane == first, 65536.0, 0.0) + jnp.where(lane == second, 131072.0, 0.0)
    code = (valid_row + marks).astype(I32)
    for q in range(n):
        note_out[q] = code[q : q + 1, :]
    first_back, second_back = targets_of(-1)
    note_in[0] = jnp.zeros((1, slots), I32)
    sum_in[pl.ds(0, 2)] = jnp.zeros((2, rows, HD), jnp.int16)
    stat_in[0] = jnp.zeros((1, 2 * 2 * rows), F32)

    pl.semaphore_wait(barrier, n - 1 + tp - 1)

    def note_copy(q):
        return pltpu.make_async_remote_copy(
            src_ref=note_out.at[q], dst_ref=note_in.at[q], send_sem=note_send, recv_sem=note_recv,
            device_id=(ahead(q), lane_me), device_id_type=MESH,
        )

    def send_note(step, carry):
        note_copy(order(step)).start()
        return carry

    lax.fori_loop(0, n - 1, send_note, 0)

    def spread(i, carry):
        for h in range(heads):
            qf[pl.ds(i * rows + h, steps, stride=heads), :] = q_ref[i, :, h * HD : (h + 1) * HD].astype(F32)
        return carry

    lax.fori_loop(0, requests, spread, 0)

    def narrow(i, carry):
        qb[i] = qf[pl.ds(pl.multiple_of(i * rows, rows), rows), :].astype(BF16)
        return carry

    lax.fori_loop(0, requests, narrow, 0)

    def wait_all(buffer, sem, count):
        pltpu.make_async_copy(buffer.at[pl.ds(1, count)], buffer.at[pl.ds(1, count)], sem).wait()

    wait_all(note_in, note_recv, n - 1)

    got = note_in[...].reshape(n, slots)
    mark = got >> 16
    count = (got & 65535).astype(F32)
    place_0 = jnp.sum(jnp.where(mark == 1, place_row + 1.0, 0.0), axis=1, keepdims=True) - 1.0
    place_1 = jnp.sum(jnp.where(mark == 2, place_row + 1.0, 0.0), axis=1, keepdims=True) - 1.0
    valid_0 = jnp.sum(jnp.where(lane == first_back, count, 0.0), axis=1, keepdims=True)
    valid_1 = jnp.sum(jnp.where(lane == second_back, count, 0.0), axis=1, keepdims=True)
    caps[0, 0:n] = jnp.where(lane < valid_0, HUGE, MASKED)
    caps[1, 0:n] = jnp.where((lane >= float(page)) & (lane < valid_1 + float(page)), HUGE, MASKED)

    line = (n, 2 * n)
    lane_2 = iota(line, 1)
    distance = iota(line, 0)
    request_0 = jnp.maximum(place_0, 0.0) - jnp.where(place_0 >= float(requests), float(requests), 0.0)
    request_1 = jnp.maximum(place_1, 0.0) - jnp.where(place_1 >= float(requests), float(requests), 0.0)
    request_row = jnp.sum(
        jnp.where(lane_2 == distance, request_0, 0.0) + jnp.where(lane_2 == distance + n, request_1, 0.0),
        axis=0, keepdims=True,
    )
    by_place = (n, HD)
    place_lane = iota(by_place, 1).astype(F32)
    distance_2 = 2.0 * iota(by_place, 0).astype(F32)
    origin_row = jnp.sum(
        jnp.where(place_lane == place_0, distance_2 + 1.0, 0.0) + jnp.where(place_lane == place_1, distance_2 + 2.0, 0.0),
        axis=0, keepdims=True,
    )
    lists[...] = jnp.zeros(lists.shape, I32)
    lists[0:1, 0 : 2 * n] = source_row.astype(I32)
    lists[1:2, 0 : 2 * n] = request_row.astype(I32)
    lists[2:3, :] = origin_row.astype(I32)
    list_copy = pltpu.make_async_copy(lists, lists_s, list_sem)
    list_copy.start()
    list_copy.wait()

    def listed(line, at, limit):
        return jnp.minimum(jnp.maximum(lists_s[line, at], 0), limit)

    def q_copy(q):
        return pltpu.make_async_remote_copy(
            src_ref=q_out.at[q], dst_ref=q_in.at[q], send_sem=q_send, recv_sem=q_recv.at[q],
            device_id=(behind(q), lane_me), device_id_type=MESH,
        )

    def send_queries(step, carry):
        q = order(step)
        q_out[q, 0:rows] = qb[listed(1, q, requests - 1)]
        q_out[q, rows : 2 * rows] = qb[listed(1, q + n, requests - 1)]
        q_copy(q).start()
        return carry

    lax.fori_loop(0, n - 1, send_queries, 0)

    for copy in pool_copies:
        copy.wait()
    tall = (2 * rows, HD)
    upper = iota(tall, 0) < rows
    key_lane = iota(tall, 1)

    def own_pages(i, carry):
        context = context_s[i]
        limit_0 = jnp.minimum(context, page)
        allowed = (upper & (key_lane < limit_0)) | ((~upper) & (key_lane >= page) & (key_lane < context))
        pages = (table_s[0, i], table_s[1, i])
        mine = qb[i]
        maxima, totals, sums = block_sums(
            jnp.concatenate([mine, mine], axis=0),
            jnp.concatenate([kv[pages[0]], kv[pages[1]]], axis=0),
            jnp.concatenate([vv[pages[0]], vv[pages[1]]], axis=0),
            jnp.where(allowed, HUGE, MASKED),
        )
        near[i] = sums / totals
        near_log[i] = jnp.broadcast_to(maxima + jnp.log(totals), tall)
        return carry

    lax.fori_loop(0, requests, own_pages, 0)

    for i in range(requests):
        nk[i * steps : (i + 1) * steps, :] = nk_ref[i].astype(F32)
        nv[i * steps : (i + 1) * steps, :] = nv_ref[i].astype(F32)
    draft_keys = nk[...].astype(BF16)
    draft_values = nv[...].astype(BF16)
    chunk = HD // rows
    blocky = (HD, HD)
    key_at = iota(blocky, 1)
    row_at = iota(blocky, 0)

    def own_draft(c, carry):
        request = c * chunk + row_at // rows
        allowed = (key_at // steps == request) & (key_at % steps <= (row_at % rows) // heads)
        block = qb[pl.ds(c * chunk, chunk)].reshape(HD, HD)
        maxima, totals, sums = block_sums(block, draft_keys, draft_values, jnp.where(allowed, HUGE, MASKED))
        at = pl.ds(pl.multiple_of(c * HD, HD), HD)
        draft[at, :] = sums / totals
        draft_log[at, :] = jnp.broadcast_to(maxima + jnp.log(totals), blocky)
        return carry

    lax.fori_loop(0, requests // chunk, own_draft, 0)

    def sum_copy(q):
        return pltpu.make_async_remote_copy(
            src_ref=sum_out.at[pl.ds(2 * q, 2)], dst_ref=sum_in.at[pl.ds(2 * q, 2)], send_sem=sum_send, recv_sem=sum_recv,
            device_id=(ahead(q), lane_me), device_id_type=MESH,
        )

    def stat_copy(q):
        return pltpu.make_async_remote_copy(
            src_ref=stat_out.at[q], dst_ref=stat_in.at[q], send_sem=stat_send, recv_sem=stat_recv,
            device_id=(ahead(q), lane_me), device_id_type=MESH,
        )

    stat_row = iota(tall, 0)

    def serve(step, carry):
        q = order(step)
        back = opposite(q)
        q_copy(q).wait_recv()
        pages = (listed(0, q, slots - 1), listed(0, q + n, slots - 1))
        cap = jnp.where(upper, caps[0, pl.ds(back, 1), :], caps[1, pl.ds(back, 1), :])
        maxima, totals, sums = block_sums(
            q_in[q],
            jnp.concatenate([kv[pages[0]], kv[pages[1]]], axis=0),
            jnp.concatenate([vv[pages[0]], vv[pages[1]]], axis=0),
            cap,
        )
        largest = jnp.maximum(jnp.max(jnp.abs(sums), axis=1, keepdims=True), 1e-30)
        coded = jnp.round(sums * (TOP / largest)).astype(I32).astype(jnp.int16)
        sum_out[2 * q] = coded[0:rows]
        sum_out[2 * q + 1] = coded[rows : 2 * rows]
        logs = maxima + jnp.log(totals)
        factor = largest / (TOP * totals)
        stat_out[q] = jnp.sum(
            jnp.where(key_lane == stat_row, logs, 0.0) + jnp.where(key_lane == stat_row + 2 * rows, factor, 0.0),
            axis=0, keepdims=True,
        )
        sum_copy(q).start()
        stat_copy(q).start()
        return carry

    lax.fori_loop(0, n - 1, serve, 0)

    def wait_sums(buffer, sem):
        view = buffer.at[pl.ds(2, 2 * n - 2)]
        pltpu.make_async_copy(view, view, sem).wait()

    wait_sums(sum_in, sum_recv)
    wait_all(stat_in, stat_recv, n - 1)

    short = (rows, HD)
    skew = iota(short, 1) - iota(short, 0)

    def combine(i, carry):
        means, logs = [], []
        for p in range(2):
            origin = listed(2, p * requests + i, 2 * n)
            away = jnp.maximum(origin - 1, 0)
            k = lax.rem(away, 2)
            stats = stat_in[lax.div(away, 2)]
            log = jnp.sum(jnp.where(skew == k * rows, stats, 0.0), axis=1, keepdims=True)
            factor = jnp.sum(jnp.where(skew == (k + 2) * rows, stats, 0.0), axis=1, keepdims=True)
            mean = sum_in[away].astype(F32) * factor
            at = pl.ds(p * rows, rows)
            means.append(jnp.where(origin > 0, mean, near[i, at]))
            logs.append(jnp.where(origin > 0, log, near_log[i, at]))
        at = pl.ds(pl.multiple_of(i * rows, rows), rows)
        means.append(draft[at, :])
        logs.append(draft_log[at, :])
        largest = jnp.maximum(jnp.maximum(logs[0], logs[1]), logs[2])
        factors = [jnp.exp(log - largest) for log in logs]
        numerator = factors[0] * means[0] + factors[1] * means[1] + factors[2] * means[2]
        result = numerator / (factors[0] + factors[1] + factors[2])
        attention[at, :] = result
        squares[i] = jnp.sum((result * result).reshape(steps, heads, HD), axis=1)
        return carry

    lax.fori_loop(0, requests, combine, 0)

    tokens = requests * steps
    total_c = jnp.sum(squares[...].reshape(tokens, HD), axis=1, keepdims=True)
    norm_rows[0] = to_row(total_c, tokens)

    def norm_copy(other):
        return pltpu.make_async_remote_copy(
            src_ref=norm_rows.at[0], dst_ref=norm_rows.at[other], send_sem=norm_send.at[other], recv_sem=norm_recv.at[other],
            device_id=(me, lax.rem(lane_me + other, tp)), device_id_type=MESH,
        )

    for other in range(1, tp):
        norm_copy(other).start()
    for other in range(1, tp):
        norm_copy(other).wait_recv()
    total = norm_rows[0]
    for other in range(1, tp):
        total = total + norm_rows[other]
    scale = lax.rsqrt(total * (1.0 / (tp * width)) + 1e-05)
    scales[...] = jnp.broadcast_to(to_column(scale, tokens), (tokens, HD)).reshape(requests, steps, HD)

    def finish(i, carry):
        for h in range(heads):
            at = slice(h * HD, (h + 1) * HD)
            out_ref[i, :, at] = attention[pl.ds(i * rows + h, steps, stride=heads), :] * scales[i] * gain_ref[:, at]
        return carry

    lax.fori_loop(0, requests, finish, 0)

    for other in range(1, tp):
        norm_copy(other).wait_send()
    wait_all(note_out, note_send, n - 1)
    wait_all(q_out, q_send, n - 1)
    wait_sums(sum_out, sum_send)
    wait_all(stat_out, stat_send, n - 1)


def per_device(n, nz, tp, queries, new_keys, new_values, key_pool, value_pool, block_table, context, source, replica, target, gain):
    requests, steps, width = queries.shape
    rows = steps * width // HD
    slots, page, _ = key_pool.shape
    entries = source.shape[0]
    vmem = pl.BlockSpec(memory_space=pltpu.VMEM)
    smem = pl.BlockSpec(memory_space=pltpu.SMEM)
    anywhere = pl.BlockSpec(memory_space=pl.ANY)
    dma = pltpu.SemaphoreType.DMA
    table = block_table.T
    return pl.pallas_call(
        functools.partial(kernel, n, nz, tp),
        out_shape=jax.ShapeDtypeStruct((requests, steps, width), F32),
        in_specs=[smem, smem, vmem, vmem, vmem, anywhere, anywhere] + [vmem] * 6,
        out_specs=vmem,
        scratch_shapes=[
            pltpu.VMEM((slots, page, HD), BF16),
            pltpu.VMEM((slots, page, HD), BF16),
            pltpu.VMEM(((requests + 1) * rows, HD), F32),
            pltpu.VMEM((requests, rows, HD), BF16),
            pltpu.VMEM((requests * steps, HD), F32),
            pltpu.VMEM((requests * steps, HD), F32),
            pltpu.VMEM((n, 1, slots), I32),
            pltpu.VMEM((n, 1, slots), I32),
            pltpu.VMEM((8, HD), I32),
            pltpu.SMEM((8, HD), I32),
            pltpu.VMEM((2, n + 8, slots), F32),
            pltpu.VMEM((n, 2 * rows, HD), BF16),
            pltpu.VMEM((n, 2 * rows, HD), BF16),
            pltpu.VMEM((2 * n, rows, HD), jnp.int16),
            pltpu.VMEM((2 * n, rows, HD), jnp.int16),
            pltpu.VMEM((n, 1, HD), F32),
            pltpu.VMEM((n, 1, HD), F32),
            pltpu.VMEM((requests, 2 * rows, HD), F32),
            pltpu.VMEM((requests, 2 * rows, HD), F32),
            pltpu.VMEM((requests * rows, HD), F32),
            pltpu.VMEM((requests * rows, HD), F32),
            pltpu.VMEM(((requests + 1) * rows, HD), F32),
            pltpu.VMEM((requests, steps, HD), F32),
            pltpu.VMEM((requests, steps, HD), F32),
            pltpu.VMEM((tp, 1, HD), F32),
            dma((2,)), dma, dma, dma, dma, dma((n,)), dma, dma, dma, dma, dma((tp,)), dma((tp,)),
        ],
        compiler_params=pltpu.CompilerParams(collective_id=0, has_side_effects=True, vmem_limit_bytes=40 * 2**20),
    )(
        table, context, queries, new_keys, new_values, key_pool, value_pool, table,
        context.reshape(1, requests), source.reshape(1, entries), replica.reshape(1, entries), target.reshape(1, entries),
        gain.reshape(1, width),
    )


def solution(mesh):
    n, tp = mesh.shape["rep"], mesh.shape["tp"]
    nz = 2 ** (n.bit_length() // 2)
    heads, replicas = P("rep", None, "tp"), P("rep")
    return jax.shard_map(
        functools.partial(per_device, n, nz, tp),
        mesh=mesh,
        in_specs=(heads, heads, heads, heads, heads, P("rep", None), replicas, replicas, replicas, replicas, P("tp")),
        out_specs=heads,
        check_vma=False,
    )
```

```python
import functools
import math

import jax
import jax.numpy as jnp
from jax import lax
from jax.experimental import pallas as pl
from jax.experimental.pallas import tpu as pltpu
from jax.sharding import PartitionSpec as P

HD = 128
MASKED = -1e30
HUGE = 3e38
TOP = 32767.0
OWN = 4
SERVE = 4
COMBINE = 4
MESH = pl.DeviceIdType.MESH
I32 = jnp.int32
F32 = jnp.float32
BF16 = jnp.bfloat16


def iota(shape, dim):
    return lax.broadcasted_iota(I32, shape, dim)


def to_column(row, size):
    shape = (size, size)
    return jnp.sum(jnp.where(iota(shape, 0) == iota(shape, 1), row, 0.0), axis=1, keepdims=True)


def to_row(column, size):
    shape = (size, size)
    return jnp.sum(jnp.where(iota(shape, 0) == iota(shape, 1), column, 0.0), axis=0, keepdims=True)


def column_sums(queries, keys, values, limit):
    page = keys[0].shape[0]
    rows = HD // len(keys)
    shape = (page, HD)
    slot = iota(shape, 1) // rows
    products = [
        lax.dot_general(key, queries, (((1,), (1,)), ((), ())), preferred_element_type=F32) for key in keys
    ]
    scores = products[0]
    for b in range(1, len(keys)):
        scores = jnp.where(slot == b, products[b], scores)
    scores = jnp.where(iota(shape, 0).astype(F32) < limit, scores * (1.0 / math.sqrt(HD)), MASKED)
    maxima = jnp.max(scores, axis=0, keepdims=True)
    weights = jnp.exp(scores - maxima)
    totals = jnp.sum(weights, axis=0, keepdims=True)
    turned = weights.T.astype(BF16)
    sums = [
        jnp.dot(turned[b * rows : (b + 1) * rows], values[b], preferred_element_type=F32) for b in range(len(keys))
    ]
    return maxima, totals, jnp.concatenate(sums, axis=0)


def block_sums(queries, keys, values, caps):
    scores = lax.dot_general(queries, keys, (((1,), (1,)), ((), ())), preferred_element_type=F32)
    scores = jnp.minimum(scores * (1.0 / math.sqrt(HD)), caps)
    maxima = jnp.max(scores, axis=1, keepdims=True)
    weights = jnp.exp(scores - maxima)
    totals = jnp.sum(weights, axis=1, keepdims=True)
    sums = jnp.dot(weights.astype(BF16), values, preferred_element_type=F32)
    return maxima, totals, sums


def kernel(
    n, nz, tp,
    q_hbm, nk_hbm, nv_hbm, kp_ref, vp_ref, table_hbm, context_hbm, source_hbm, replica_hbm, target_hbm, gain_hbm,
    out_ref,
    table_s, context_s, q_ref, nk_ref, nv_ref, table_ref, context_ref, source_ref, replica_ref, target_ref, gain_ref,
    kv, vv, qf, qb, nk, nv,
    note_out, note_in, lists, lists_s, limits,
    q_out, q_in, sum_out, sum_in, stat_out, stat_in,
    near, near_stat, draft, draft_log, attention, squares, scales, norm_rows,
    in_sem, list_sem, note_send, note_recv, q_send, q_recv, sum_send, sum_recv, stat_send, stat_recv, norm_send, norm_recv,
):
    ny = n // nz
    requests, steps, width = q_hbm.shape
    heads = width // HD
    rows = steps * heads
    entries = replica_hbm.shape[1]
    slots = kp_ref.shape[0]
    page = kp_ref.shape[1]
    me = lax.axis_index("rep")
    lane_me = lax.axis_index("tp")
    my, mz = lax.div(me, nz), lax.rem(me, nz)

    def ahead(q):
        return lax.rem(my + lax.div(q, nz), ny) * nz + lax.rem(mz + lax.rem(q, nz), nz)

    def behind(q):
        return lax.rem(my + ny - lax.div(q, nz), ny) * nz + lax.rem(mz + nz - lax.rem(q, nz), nz)

    def opposite(q):
        return lax.rem(ny - lax.div(q, nz), ny) * nz + lax.rem(nz - lax.rem(q, nz), nz)

    def order(step):
        return lax.rem((step + 1) * 27, n)

    moves = [
        (replica_hbm, replica_ref), (source_hbm, source_ref), (target_hbm, target_ref), (table_hbm, table_ref),
        (context_hbm, context_ref), (q_hbm, q_ref), (table_hbm, table_s), (context_hbm, context_s), (nk_hbm, nk_ref),
        (nv_hbm, nv_ref), (kp_ref, kv), (vp_ref, vv), (gain_hbm, gain_ref),
    ]
    fetches = [pltpu.make_async_copy(a, b, in_sem.at[at]) for at, (a, b) in enumerate(moves)]
    for fetch in fetches:
        fetch.start()

    barrier = pltpu.get_barrier_semaphore()

    def greet(step, carry):
        pl.semaphore_signal(barrier, inc=1, device_id=(ahead(step + 1), lane_me), device_id_type=MESH)
        return carry

    lax.fori_loop(0, n - 1, greet, 0)
    for other in range(1, tp):
        pl.semaphore_signal(barrier, inc=1, device_id=(me, lax.rem(lane_me + other, tp)), device_id_type=MESH)

    for fetch in fetches[0:5]:
        fetch.wait()

    replica = replica_ref[...].astype(F32)
    source = source_ref[...].astype(F32)
    target = target_ref[...].astype(F32)
    square = (entries, entries)
    replica_c = to_column(replica, entries)
    same_before = (replica_c == replica) & (iota(square, 0) < iota(square, 1))
    rank = jnp.sum(jnp.where(same_before, 1.0, 0.0), axis=0, keepdims=True)
    rank_c = to_column(rank, entries)
    source_c = to_column(source, entries)

    def vector_peer(q, sign):
        dy, dz = q // nz, q % nz
        return (((my + ny + sign * dy) % ny) * nz + (mz + nz + sign * dz) % nz).astype(F32)

    def targets_of(sign):
        peers = vector_peer(iota((n, entries), 0), sign)
        found = []
        for k in range(2):
            chosen = (peers == replica) & (rank == float(k))
            found.append(jnp.sum(jnp.where(chosen, target + 1.0, 0.0), axis=1, keepdims=True) - 1.0)
        return found

    wide = (entries, 2 * n)
    peers_row = vector_peer(iota(wide, 1) % n, 1)
    chosen = (replica_c == peers_row) & (rank_c == (iota(wide, 1) // n).astype(F32))
    source_row = jnp.sum(jnp.where(chosen, source_c, 0.0), axis=0, keepdims=True)

    context_c = to_column(context_ref[...].astype(F32), requests)
    by_slot = (requests, slots)
    slot_lane = iota(by_slot, 1).astype(F32)
    request_c = iota(by_slot, 0).astype(F32)
    valid_row = jnp.zeros((1, slots), F32)
    place_row = jnp.zeros((1, slots), F32)
    for p in range(2):
        table_c = to_column(table_ref[p : p + 1, :].astype(F32), requests)
        here = table_c == slot_lane
        valid = jnp.clip(context_c - float(p * page), 0.0, float(page))
        valid_row += jnp.sum(jnp.where(here, valid, 0.0), axis=0, keepdims=True)
        place_row += jnp.sum(jnp.where(here, request_c + float(p * requests), 0.0), axis=0, keepdims=True)

    notes = (n, slots)
    lane = iota(notes, 1).astype(F32)
    first, second = targets_of(1)
    marks = jnp.where(lane == first, 65536.0, 0.0) + jnp.where(lane == second, 131072.0, 0.0)
    code = (valid_row + marks).astype(I32)
    for q in range(n):
        note_out[q] = code[q : q + 1, :]
    first_back, second_back = targets_of(-1)
    note_in[0] = jnp.zeros((1, slots), I32)
    q_in[0] = jnp.zeros((2 * rows, HD), BF16)
    sum_in[pl.ds(0, 2)] = jnp.zeros((2, rows, HD), jnp.int16)
    stat_in[0] = jnp.zeros((1, 2 * 2 * rows), F32)

    pl.semaphore_wait(barrier, n - 1 + tp - 1)

    def note_copy(q):
        return pltpu.make_async_remote_copy(
            src_ref=note_out.at[q], dst_ref=note_in.at[q], send_sem=note_send, recv_sem=note_recv,
            device_id=(ahead(q), lane_me), device_id_type=MESH,
        )

    def send_note(step, carry):
        note_copy(order(step)).start()
        return carry

    lax.fori_loop(0, n - 1, send_note, 0)

    fetches[5].wait()

    def spread(i, carry):
        for h in range(heads):
            qf[pl.ds(i * rows + h, steps, stride=heads), :] = q_ref[i, :, h * HD : (h + 1) * HD].astype(F32)
        return carry

    lax.fori_loop(0, requests, spread, 0)

    def narrow(i, carry):
        qb[i] = qf[pl.ds(pl.multiple_of(i * rows, rows), rows), :].astype(BF16)
        return carry

    lax.fori_loop(0, requests, narrow, 0)

    def wait_all(buffer, sem, count):
        pltpu.make_async_copy(buffer.at[pl.ds(1, count)], buffer.at[pl.ds(1, count)], sem).wait()

    wait_all(note_in, note_recv, n - 1)

    got = note_in[...].reshape(n, slots)
    mark = got >> 16
    count = (got & 65535).astype(F32)
    place_0 = jnp.sum(jnp.where(mark == 1, place_row + 1.0, 0.0), axis=1, keepdims=True) - 1.0
    place_1 = jnp.sum(jnp.where(mark == 2, place_row + 1.0, 0.0), axis=1, keepdims=True) - 1.0
    valid_0 = jnp.sum(jnp.where(lane == first_back, count, 0.0), axis=1, keepdims=True)
    valid_1 = jnp.sum(jnp.where(lane == second_back, count, 0.0), axis=1, keepdims=True)
    half = lane - jnp.where(lane >= float(2 * rows), float(2 * rows), 0.0)
    limits[0:n] = jnp.where(half < float(rows), valid_0, valid_1)

    line = (n, 2 * n)
    lane_2 = iota(line, 1)
    distance = iota(line, 0)
    request_0 = jnp.maximum(place_0, 0.0) - jnp.where(place_0 >= float(requests), float(requests), 0.0)
    request_1 = jnp.maximum(place_1, 0.0) - jnp.where(place_1 >= float(requests), float(requests), 0.0)
    request_row = jnp.sum(
        jnp.where(lane_2 == distance, request_0, 0.0) + jnp.where(lane_2 == distance + n, request_1, 0.0),
        axis=0, keepdims=True,
    )
    by_place = (n, HD)
    place_lane = iota(by_place, 1).astype(F32)
    distance_2 = 2.0 * iota(by_place, 0).astype(F32)
    origin_row = jnp.sum(
        jnp.where(place_lane == place_0, distance_2 + 1.0, 0.0) + jnp.where(place_lane == place_1, distance_2 + 2.0, 0.0),
        axis=0, keepdims=True,
    )
    lists[...] = jnp.zeros(lists.shape, I32)
    lists[0:1, 0 : 2 * n] = source_row.astype(I32)
    lists[1:2, 0 : 2 * n] = request_row.astype(I32)
    lists[2:3, :] = origin_row.astype(I32)
    list_copy = pltpu.make_async_copy(lists, lists_s, list_sem)
    list_copy.start()
    list_copy.wait()

    def listed(line, at, limit):
        return jnp.minimum(jnp.maximum(lists_s[line, at], 0), limit)

    def q_copy(q):
        return pltpu.make_async_remote_copy(
            src_ref=q_out.at[q], dst_ref=q_in.at[q], send_sem=q_send, recv_sem=q_recv.at[q],
            device_id=(behind(q), lane_me), device_id_type=MESH,
        )

    def send_queries(step, carry):
        q = order(step)
        q_out[q, 0:rows] = qb[listed(1, q, requests - 1)]
        q_out[q, rows : 2 * rows] = qb[listed(1, q + n, requests - 1)]
        q_copy(q).start()
        return carry

    lax.fori_loop(0, n - 1, send_queries, 0)

    for fetch in fetches[6:]:
        fetch.wait()
    lane_1 = iota((1, HD), 1)
    own_lane = lane_1 // rows

    def stat_pair(logs, factors):
        low = lane_1 < 2 * rows
        return (
            jnp.where(low, logs, pltpu.roll(factors, 2 * rows, axis=1)),
            jnp.where(low, pltpu.roll(logs, 2 * rows, axis=1), factors),
        )

    def own_pages(step, carry):
        pair = (2 * step, 2 * step + 1)
        first_context, second_context = context_s[0, pair[0]], context_s[0, pair[1]]
        limit = jnp.where(own_lane < 2, first_context, second_context) - jnp.where(own_lane % 2 == 1, page, 0)
        pages = [table_s[p, i] for i in pair for p in range(2)]
        mine = [qb[i] for i in pair]
        maxima, totals, sums = column_sums(
            jnp.concatenate([mine[0], mine[0], mine[1], mine[1]], axis=0),
            [kv[at] for at in pages], [vv[at] for at in pages], limit.astype(F32),
        )
        stats = stat_pair(maxima + jnp.log(totals), 1.0 / totals)
        for at, i in enumerate(pair):
            near[i] = sums[at * 2 * rows : (at + 1) * 2 * rows]
            near_stat[i] = stats[at]
        return carry

    lax.fori_loop(0, requests // 2, own_pages, 0, unroll=OWN)

    for i in range(requests):
        nk[i * steps : (i + 1) * steps, :] = nk_ref[i].astype(F32)
        nv[i * steps : (i + 1) * steps, :] = nv_ref[i].astype(F32)
    draft_keys = nk[...].astype(BF16)
    draft_values = nv[...].astype(BF16)
    chunk = HD // rows
    blocky = (HD, HD)
    key_at = iota(blocky, 1)
    row_at = iota(blocky, 0)

    def own_draft(c, carry):
        request = c * chunk + row_at // rows
        allowed = (key_at // steps == request) & (key_at % steps <= (row_at % rows) // heads)
        block = qb[pl.ds(c * chunk, chunk)].reshape(HD, HD)
        maxima, totals, sums = block_sums(block, draft_keys, draft_values, jnp.where(allowed, HUGE, MASKED))
        at = pl.ds(pl.multiple_of(c * HD, HD), HD)
        draft[at, :] = sums / totals
        draft_log[at, :] = jnp.broadcast_to(maxima + jnp.log(totals), blocky)
        return carry

    lax.fori_loop(0, requests // chunk, own_draft, 0, unroll=2)

    def sum_copy(q):
        return pltpu.make_async_remote_copy(
            src_ref=sum_out.at[pl.ds(2 * q, 2)], dst_ref=sum_in.at[pl.ds(2 * q, 2)], send_sem=sum_send, recv_sem=sum_recv,
            device_id=(ahead(q), lane_me), device_id_type=MESH,
        )

    def stat_copy(q):
        return pltpu.make_async_remote_copy(
            src_ref=stat_out.at[q], dst_ref=stat_in.at[q], send_sem=stat_send, recv_sem=stat_recv,
            device_id=(ahead(q), lane_me), device_id_type=MESH,
        )

    square_1 = iota(blocky, 0) == iota(blocky, 1)

    def serve_pair(first_q, second_q):
        pair = (first_q, second_q)
        pages = [listed(0, q + k * n, slots - 1) for q in pair for k in range(2)]
        ends = [limits[pl.ds(opposite(q), 1), :] for q in pair]
        maxima, totals, sums = column_sums(
            jnp.concatenate([q_in[q] for q in pair], axis=0),
            [kv[at] for at in pages], [vv[at] for at in pages], jnp.where(own_lane < 2, ends[0], ends[1]),
        )
        largest = jnp.maximum(jnp.max(jnp.abs(sums), axis=1, keepdims=True), 1e-30)
        coded = jnp.round(sums * (TOP / largest)).astype(I32).astype(jnp.int16)
        largest_row = jnp.sum(jnp.where(square_1, largest, 0.0), axis=0, keepdims=True)
        stats = stat_pair(maxima + jnp.log(totals), largest_row / (TOP * totals))
        for at, q in enumerate(pair):
            sum_out[pl.ds(2 * q, 2)] = coded[at * 2 * rows : (at + 1) * 2 * rows].reshape(2, rows, HD)
            stat_out[q] = stats[at]

    def serve(step, carry):
        qs = [order(step * SERVE + at) for at in range(SERVE)]
        for q in qs:
            q_copy(q).wait_recv()
        for at in range(0, SERVE, 2):
            serve_pair(qs[at], qs[at + 1])
        for q in qs:
            sum_copy(q).start()
            stat_copy(q).start()
        return carry

    whole = (n - 2) // SERVE
    lax.fori_loop(0, whole, serve, 0)
    rest = [order(step) for step in range(whole * SERVE, n - 1)]
    for q in rest:
        q_copy(q).wait_recv()
    for at in range(0, len(rest), 2):
        serve_pair(rest[at], rest[at + 1] if at + 1 < len(rest) else 0)
    for q in rest:
        sum_copy(q).start()
        stat_copy(q).start()

    def wait_sums(buffer, sem):
        view = buffer.at[pl.ds(2, 2 * n - 2)]
        pltpu.make_async_copy(view, view, sem).wait()

    wait_sums(sum_in, sum_recv)
    wait_all(stat_in, stat_recv, n - 1)

    short = (rows, HD)
    skew = iota(short, 1) - iota(short, 0)

    def combine(i, carry):
        means, logs = [], []
        for p in range(2):
            origin = listed(2, p * requests + i, 2 * n)
            away = jnp.maximum(origin - 1, 0)
            moved = origin > 0
            stats = jnp.where(moved, stat_in[lax.div(away, 2)], near_stat[i])
            skip = jnp.where(moved, lax.rem(away, 2), p) * rows
            logs.append(jnp.sum(jnp.where(skew == skip, stats, 0.0), axis=1, keepdims=True))
            factor = jnp.sum(jnp.where(skew == skip + 2 * rows, stats, 0.0), axis=1, keepdims=True)
            means.append(jnp.where(moved, sum_in[away].astype(F32), near[i, pl.ds(p * rows, rows)]) * factor)
        at = pl.ds(pl.multiple_of(i * rows, rows), rows)
        means.append(draft[at, :])
        logs.append(draft_log[at, :])
        largest = jnp.maximum(jnp.maximum(logs[0], logs[1]), logs[2])
        factors = [jnp.exp(log - largest) for log in logs]
        numerator = factors[0] * means[0] + factors[1] * means[1] + factors[2] * means[2]
        result = numerator / (factors[0] + factors[1] + factors[2])
        attention[at, :] = result
        squares[i] = jnp.sum((result * result).reshape(steps, heads, HD), axis=1)
        return carry

    lax.fori_loop(0, requests, combine, 0, unroll=COMBINE)

    tokens = requests * steps
    total_c = jnp.sum(squares[...].reshape(tokens, HD), axis=1, keepdims=True)
    norm_rows[0] = to_row(total_c, tokens)

    def norm_copy(other):
        return pltpu.make_async_remote_copy(
            src_ref=norm_rows.at[0], dst_ref=norm_rows.at[other], send_sem=norm_send.at[other], recv_sem=norm_recv.at[other],
            device_id=(me, lax.rem(lane_me + other, tp)), device_id_type=MESH,
        )

    for other in range(1, tp):
        norm_copy(other).start()
    for other in range(1, tp):
        norm_copy(other).wait_recv()
    total = norm_rows[0]
    for other in range(1, tp):
        total = total + norm_rows[other]
    scale = lax.rsqrt(total * (1.0 / (tp * width)) + 1e-05)
    scales[...] = jnp.broadcast_to(to_column(scale, tokens), (tokens, HD)).reshape(requests, steps, HD)

    def finish(i, carry):
        for h in range(heads):
            at = slice(h * HD, (h + 1) * HD)
            out_ref[i, :, at] = attention[pl.ds(i * rows + h, steps, stride=heads), :] * scales[i] * gain_ref[:, at]
        return carry

    lax.fori_loop(0, requests, finish, 0)

    for other in range(1, tp):
        norm_copy(other).wait_send()
    wait_all(note_out, note_send, n - 1)
    wait_all(q_out, q_send, n - 1)
    wait_sums(sum_out, sum_send)
    wait_all(stat_out, stat_send, n - 1)


def per_device(n, nz, tp, queries, new_keys, new_values, key_pool, value_pool, block_table, context, source, replica, target, gain):
    requests, steps, width = queries.shape
    rows = steps * width // HD
    slots, page, _ = key_pool.shape
    entries = source.shape[0]
    vmem = pl.BlockSpec(memory_space=pltpu.VMEM)
    anywhere = pl.BlockSpec(memory_space=pl.ANY)
    dma = pltpu.SemaphoreType.DMA
    table = block_table.T
    return pl.pallas_call(
        functools.partial(kernel, n, nz, tp),
        out_shape=jax.ShapeDtypeStruct((requests, steps, width), F32),
        in_specs=[anywhere] * 11,
        out_specs=vmem,
        scratch_shapes=[
            pltpu.SMEM((2, requests), I32),
            pltpu.SMEM((1, requests), I32),
            pltpu.VMEM((requests, steps, width), BF16),
            pltpu.VMEM((requests, steps, HD), BF16),
            pltpu.VMEM((requests, steps, HD), BF16),
            pltpu.VMEM((2, requests), I32),
            pltpu.VMEM((1, requests), I32),
            pltpu.VMEM((1, entries), I32),
            pltpu.VMEM((1, entries), I32),
            pltpu.VMEM((1, entries), I32),
            pltpu.VMEM((1, width), F32),
            pltpu.VMEM((slots, page, HD), BF16),
            pltpu.VMEM((slots, page, HD), BF16),
            pltpu.VMEM(((requests + 1) * rows, HD), F32),
            pltpu.VMEM((requests, rows, HD), BF16),
            pltpu.VMEM((requests * steps, HD), F32),
            pltpu.VMEM((requests * steps, HD), F32),
            pltpu.VMEM((n, 1, slots), I32),
            pltpu.VMEM((n, 1, slots), I32),
            pltpu.VMEM((8, HD), I32),
            pltpu.SMEM((8, HD), I32),
            pltpu.VMEM((n + 8, slots), F32),
            pltpu.VMEM((n, 2 * rows, HD), BF16),
            pltpu.VMEM((n, 2 * rows, HD), BF16),
            pltpu.VMEM((2 * n, rows, HD), jnp.int16),
            pltpu.VMEM((2 * n, rows, HD), jnp.int16),
            pltpu.VMEM((n, 1, HD), F32),
            pltpu.VMEM((n, 1, HD), F32),
            pltpu.VMEM((requests, 2 * rows, HD), F32),
            pltpu.VMEM((requests, 1, HD), F32),
            pltpu.VMEM((requests * rows, HD), F32),
            pltpu.VMEM((requests * rows, HD), F32),
            pltpu.VMEM(((requests + 1) * rows, HD), F32),
            pltpu.VMEM((requests, steps, HD), F32),
            pltpu.VMEM((requests, steps, HD), F32),
            pltpu.VMEM((tp, 1, HD), F32),
            dma((13,)), dma, dma, dma, dma, dma((n,)), dma, dma, dma, dma, dma((tp,)), dma((tp,)),
        ],
        compiler_params=pltpu.CompilerParams(collective_id=0, has_side_effects=True, vmem_limit_bytes=56 * 2**20),
    )(
        queries, new_keys, new_values, key_pool, value_pool, table,
        context.reshape(1, requests), source.reshape(1, entries), replica.reshape(1, entries), target.reshape(1, entries),
        gain.reshape(1, width),
    )


def solution(mesh):
    n, tp = mesh.shape["rep"], mesh.shape["tp"]
    nz = 2 ** (n.bit_length() // 2)
    heads, replicas = P("rep", None, "tp"), P("rep")
    return jax.shard_map(
        functools.partial(per_device, n, nz, tp),
        mesh=mesh,
        in_specs=(heads, heads, heads, heads, heads, P("rep", None), replicas, replicas, replicas, replicas, P("tp")),
        out_specs=heads,
        check_vma=False,
    )
```

```python
import functools
import math

import jax
import jax.numpy as jnp
from jax import lax
from jax.experimental import pallas as pl
from jax.experimental.pallas import tpu as pltpu
from jax.sharding import PartitionSpec as P

HD = 128
MASKED = -1e30
HUGE = 3e38
TOP = 32767.0
OWN = 4
SERVE = 4
COMBINE = 4
MESH = pl.DeviceIdType.MESH
I32 = jnp.int32
F32 = jnp.float32
BF16 = jnp.bfloat16


def iota(shape, dim):
    return lax.broadcasted_iota(I32, shape, dim)


def to_column(row, size):
    shape = (size, size)
    return jnp.sum(jnp.where(iota(shape, 0) == iota(shape, 1), row, 0.0), axis=1, keepdims=True)


def to_row(column, size):
    shape = (size, size)
    return jnp.sum(jnp.where(iota(shape, 0) == iota(shape, 1), column, 0.0), axis=0, keepdims=True)


def column_sums(queries, keys, values, limit):
    page = keys[0].shape[0]
    rows = HD // len(keys)
    shape = (page, HD)
    slot = iota(shape, 1) // rows
    products = [
        lax.dot_general(key, queries, (((1,), (1,)), ((), ())), preferred_element_type=F32) for key in keys
    ]
    scores = products[0]
    for b in range(1, len(keys)):
        scores = jnp.where(slot == b, products[b], scores)
    scores = jnp.where(iota(shape, 0).astype(F32) < limit, scores * (1.0 / math.sqrt(HD)), MASKED)
    maxima = jnp.max(scores, axis=0, keepdims=True)
    weights = jnp.exp(scores - maxima)
    totals = jnp.sum(weights, axis=0, keepdims=True)
    turned = weights.T.astype(BF16)
    sums = [
        jnp.dot(turned[b * rows : (b + 1) * rows], values[b], preferred_element_type=F32) for b in range(len(keys))
    ]
    return maxima, totals, jnp.concatenate(sums, axis=0)


def block_sums(queries, keys, values, caps):
    scores = lax.dot_general(queries, keys, (((1,), (1,)), ((), ())), preferred_element_type=F32)
    scores = jnp.minimum(scores * (1.0 / math.sqrt(HD)), caps)
    maxima = jnp.max(scores, axis=1, keepdims=True)
    weights = jnp.exp(scores - maxima)
    totals = jnp.sum(weights, axis=1, keepdims=True)
    sums = jnp.dot(weights.astype(BF16), values, preferred_element_type=F32)
    return maxima, totals, sums


def kernel(
    n, nz, tp,
    q_hbm, nk_hbm, nv_hbm, kp_ref, vp_ref, table_hbm, context_hbm, source_hbm, replica_hbm, target_hbm, gain_hbm,
    out_ref,
    table_s, context_s, q_ref, nk_ref, nv_ref, table_ref, context_ref, source_ref, replica_ref, target_ref, gain_ref,
    kv, vv, qf, qb, nk, nv,
    info, lists, lists_s, limits,
    q_out, q_in, sum_out, sum_in, stat_out, stat_in,
    near, near_stat, draft, draft_log, attention, squares, scales, norm_rows,
    in_sem, list_sem, row_send, row_recv, column_send, column_recv, q_send, q_recv, sum_send, sum_recv, stat_send, stat_recv, norm_send, norm_recv,
):
    ny = n // nz
    requests, steps, width = q_hbm.shape
    heads = width // HD
    rows = steps * heads
    entries = replica_hbm.shape[1]
    slots = kp_ref.shape[0]
    page = kp_ref.shape[1]
    me = lax.axis_index("rep")
    lane_me = lax.axis_index("tp")
    my, mz = lax.div(me, nz), lax.rem(me, nz)

    def ahead(q):
        return lax.rem(my + lax.div(q, nz), ny) * nz + lax.rem(mz + lax.rem(q, nz), nz)

    def behind(q):
        return lax.rem(my + ny - lax.div(q, nz), ny) * nz + lax.rem(mz + nz - lax.rem(q, nz), nz)

    def around(base, step, size):
        total = base + step
        return jnp.where(total >= size, total - size, total)

    def order(step):
        return lax.rem((step + 1) * 27, n)

    moves = [
        (replica_hbm, replica_ref), (source_hbm, source_ref), (target_hbm, target_ref), (table_hbm, table_ref),
        (context_hbm, context_ref), (q_hbm, q_ref), (table_hbm, table_s), (context_hbm, context_s), (nk_hbm, nk_ref),
        (nv_hbm, nv_ref), (kp_ref, kv), (vp_ref, vv), (gain_hbm, gain_ref),
    ]
    fetches = [pltpu.make_async_copy(a, b, in_sem.at[at]) for at, (a, b) in enumerate(moves)]
    for fetch in fetches:
        fetch.start()

    barrier = pltpu.get_barrier_semaphore()
    for other in range(1, nz):
        pl.semaphore_signal(barrier, inc=1, device_id=(my * nz + around(mz, other, nz), lane_me), device_id_type=MESH)
    for other in range(1, ny):
        pl.semaphore_signal(barrier, inc=1, device_id=(around(my, other, ny) * nz + mz, lane_me), device_id_type=MESH)
    for other in range(1, tp):
        pl.semaphore_signal(barrier, inc=1, device_id=(me, around(lane_me, other, tp)), device_id_type=MESH)

    for fetch in fetches[0:5]:
        fetch.wait()

    info[my, mz] = jnp.full((2, HD), -1, I32)
    info[my, mz, 0:1, 0:entries] = replica_ref[...] * 65536 + target_ref[...]
    context_c = to_column(context_ref[...].astype(F32), requests)
    by_slot = (requests, slots)
    slot_lane = iota(by_slot, 1).astype(F32)
    request_c = iota(by_slot, 0).astype(F32)
    valid_row = jnp.zeros((1, slots), F32)
    place_row = jnp.zeros((1, slots), F32)
    for p in range(2):
        table_c = to_column(table_ref[p : p + 1, :].astype(F32), requests)
        here = table_c == slot_lane
        valid = jnp.clip(context_c - float(p * page), 0.0, float(page))
        valid_row += jnp.sum(jnp.where(here, valid, 0.0), axis=0, keepdims=True)
        place_row += jnp.sum(jnp.where(here, request_c + float(p * requests), 0.0), axis=0, keepdims=True)

    info[my, mz, 1:2, 0:slots] = valid_row.astype(I32)
    q_in[0] = jnp.zeros((2 * rows, HD), BF16)
    sum_in[pl.ds(0, 2)] = jnp.zeros((2, rows, HD), jnp.int16)
    stat_in[0] = jnp.zeros((1, 2 * 2 * rows), F32)

    pl.semaphore_wait(barrier, nz - 1 + ny - 1 + tp - 1)

    def row_copy(other, at):
        return pltpu.make_async_remote_copy(
            src_ref=info.at[my, at], dst_ref=info.at[my, at], send_sem=row_send.at[other], recv_sem=row_recv.at[other],
            device_id=(my * nz + around(mz, other, nz), lane_me), device_id_type=MESH,
        )

    def column_copy(other, at):
        return pltpu.make_async_remote_copy(
            src_ref=info.at[at], dst_ref=info.at[at], send_sem=column_send.at[other], recv_sem=column_recv.at[other],
            device_id=(around(my, other, ny) * nz + mz, lane_me), device_id_type=MESH,
        )

    for other in range(1, nz):
        row_copy(other, mz).start()

    replica = replica_ref[...].astype(F32)
    source = source_ref[...].astype(F32)
    target = target_ref[...].astype(F32)
    square = (entries, entries)
    replica_c = to_column(replica, entries)
    same_before = (replica_c == replica) & (iota(square, 0) < iota(square, 1))
    rank = jnp.sum(jnp.where(same_before, 1.0, 0.0), axis=0, keepdims=True)
    rank_c = to_column(rank, entries)
    source_c = to_column(source, entries)
    wide = (entries, 2 * n)
    chosen = (replica_c == (iota(wide, 1) % n).astype(F32)) & (rank_c == (iota(wide, 1) // n).astype(F32))
    source_row = jnp.sum(jnp.where(chosen, source_c, 0.0), axis=0, keepdims=True)
    receiver = iota((n, entries), 0).astype(F32)
    landings = []
    for k in range(2):
        chosen = (receiver == replica) & (rank == float(k))
        landings.append(jnp.sum(jnp.where(chosen, target + 1.0, 0.0), axis=1, keepdims=True) - 1.0)

    for other in range(1, nz):
        row_copy(other, around(mz, nz - other, nz)).wait_recv()
    for other in range(1, ny):
        column_copy(other, my).start()

    fetches[5].wait()

    def spread(i, carry):
        for h in range(heads):
            qf[pl.ds(i * rows + h, steps, stride=heads), :] = q_ref[i, :, h * HD : (h + 1) * HD].astype(F32)
        return carry

    lax.fori_loop(0, requests, spread, 0)

    def narrow(i, carry):
        qb[i] = qf[pl.ds(pl.multiple_of(i * rows, rows), rows), :].astype(BF16)
        return carry

    lax.fori_loop(0, requests, narrow, 0)

    def wait_all(buffer, sem, count):
        pltpu.make_async_copy(buffer.at[pl.ds(1, count)], buffer.at[pl.ds(1, count)], sem).wait()

    for other in range(1, ny):
        column_copy(other, around(my, ny - other, ny)).wait_recv()

    words = info[:, :, 0, :].reshape(n, HD)
    count = info[:, :, 1, 0:slots].reshape(n, slots).astype(F32)
    place = iota((n, HD), 1)
    sender = iota((n, HD), 0)
    here = ((words >> 16) == me) & (sender != me)
    keyed = (place * 256 + (words & 65535)).astype(F32)
    first = jnp.min(jnp.where(here, keyed, 1e6), axis=1, keepdims=True)
    last = jnp.max(jnp.where(here, keyed, -1.0), axis=1, keepdims=True)
    slot_0 = jnp.where(last >= 0.0, first - 256.0 * jnp.floor(first * (1.0 / 256.0)), -1.0)
    slot_1 = jnp.where(last > first, last - 256.0 * jnp.floor(last * (1.0 / 256.0)), -1.0)
    lane = iota((n, slots), 1).astype(F32)
    place_0 = jnp.sum(jnp.where(lane == slot_0, place_row + 1.0, 0.0), axis=1, keepdims=True) - 1.0
    place_1 = jnp.sum(jnp.where(lane == slot_1, place_row + 1.0, 0.0), axis=1, keepdims=True) - 1.0
    valid_0 = jnp.sum(jnp.where(lane == landings[0], count, 0.0), axis=1, keepdims=True)
    valid_1 = jnp.sum(jnp.where(lane == landings[1], count, 0.0), axis=1, keepdims=True)
    half = lane - jnp.where(lane >= float(2 * rows), float(2 * rows), 0.0)
    limits[0:n] = jnp.where(half < float(rows), valid_0, valid_1)

    line = (n, 2 * n)
    lane_2 = iota(line, 1)
    distance = iota(line, 0)
    request_0 = jnp.maximum(place_0, 0.0) - jnp.where(place_0 >= float(requests), float(requests), 0.0)
    request_1 = jnp.maximum(place_1, 0.0) - jnp.where(place_1 >= float(requests), float(requests), 0.0)
    request_row = jnp.sum(
        jnp.where(lane_2 == distance, request_0, 0.0) + jnp.where(lane_2 == distance + n, request_1, 0.0),
        axis=0, keepdims=True,
    )
    by_place = (n, HD)
    place_lane = iota(by_place, 1).astype(F32)
    holder = iota(by_place, 0)
    distance_2 = 2.0 * (((my + ny - holder // nz) % ny) * nz + (mz + nz - holder % nz) % nz).astype(F32)
    origin_row = jnp.sum(
        jnp.where(place_lane == place_0, distance_2 + 1.0, 0.0) + jnp.where(place_lane == place_1, distance_2 + 2.0, 0.0),
        axis=0, keepdims=True,
    )
    lists[...] = jnp.zeros(lists.shape, I32)
    lists[0:1, 0 : 2 * n] = source_row.astype(I32)
    lists[1:2, 0 : 2 * n] = request_row.astype(I32)
    lists[2:3, :] = origin_row.astype(I32)
    list_copy = pltpu.make_async_copy(lists, lists_s, list_sem)
    list_copy.start()
    list_copy.wait()

    def listed(line, at, limit):
        return jnp.minimum(jnp.maximum(lists_s[line, at], 0), limit)

    def q_copy(q):
        return pltpu.make_async_remote_copy(
            src_ref=q_out.at[q], dst_ref=q_in.at[q], send_sem=q_send, recv_sem=q_recv.at[q],
            device_id=(behind(q), lane_me), device_id_type=MESH,
        )

    def send_queries(step, carry):
        q = order(step)
        holder = behind(q)
        q_out[q, 0:rows] = qb[listed(1, holder, requests - 1)]
        q_out[q, rows : 2 * rows] = qb[listed(1, holder + n, requests - 1)]
        q_copy(q).start()
        return carry

    lax.fori_loop(0, n - 1, send_queries, 0)

    for fetch in fetches[6:]:
        fetch.wait()
    lane_1 = iota((1, HD), 1)
    own_lane = lane_1 // rows

    def stat_pair(logs, factors):
        low = lane_1 < 2 * rows
        return (
            jnp.where(low, logs, pltpu.roll(factors, 2 * rows, axis=1)),
            jnp.where(low, pltpu.roll(logs, 2 * rows, axis=1), factors),
        )

    def own_pages(step, carry):
        pair = (2 * step, 2 * step + 1)
        first_context, second_context = context_s[0, pair[0]], context_s[0, pair[1]]
        limit = jnp.where(own_lane < 2, first_context, second_context) - jnp.where(own_lane % 2 == 1, page, 0)
        pages = [table_s[p, i] for i in pair for p in range(2)]
        mine = [qb[i] for i in pair]
        maxima, totals, sums = column_sums(
            jnp.concatenate([mine[0], mine[0], mine[1], mine[1]], axis=0),
            [kv[at] for at in pages], [vv[at] for at in pages], limit.astype(F32),
        )
        stats = stat_pair(maxima + jnp.log(totals), 1.0 / totals)
        for at, i in enumerate(pair):
            near[i] = sums[at * 2 * rows : (at + 1) * 2 * rows]
            near_stat[i] = stats[at]
        return carry

    lax.fori_loop(0, requests // 2, own_pages, 0, unroll=OWN)

    for i in range(requests):
        nk[i * steps : (i + 1) * steps, :] = nk_ref[i].astype(F32)
        nv[i * steps : (i + 1) * steps, :] = nv_ref[i].astype(F32)
    draft_keys = nk[...].astype(BF16)
    draft_values = nv[...].astype(BF16)
    chunk = HD // rows
    blocky = (HD, HD)
    key_at = iota(blocky, 1)
    row_at = iota(blocky, 0)

    def own_draft(c, carry):
        request = c * chunk + row_at // rows
        allowed = (key_at // steps == request) & (key_at % steps <= (row_at % rows) // heads)
        block = qb[pl.ds(c * chunk, chunk)].reshape(HD, HD)
        maxima, totals, sums = block_sums(block, draft_keys, draft_values, jnp.where(allowed, HUGE, MASKED))
        at = pl.ds(pl.multiple_of(c * HD, HD), HD)
        draft[at, :] = sums / totals
        draft_log[at, :] = jnp.broadcast_to(maxima + jnp.log(totals), blocky)
        return carry

    lax.fori_loop(0, requests // chunk, own_draft, 0, unroll=2)

    def sum_copy(q):
        return pltpu.make_async_remote_copy(
            src_ref=sum_out.at[pl.ds(2 * q, 2)], dst_ref=sum_in.at[pl.ds(2 * q, 2)], send_sem=sum_send, recv_sem=sum_recv,
            device_id=(ahead(q), lane_me), device_id_type=MESH,
        )

    def stat_copy(q):
        return pltpu.make_async_remote_copy(
            src_ref=stat_out.at[q], dst_ref=stat_in.at[q], send_sem=stat_send, recv_sem=stat_recv,
            device_id=(ahead(q), lane_me), device_id_type=MESH,
        )

    square_1 = iota(blocky, 0) == iota(blocky, 1)

    def serve_pair(first_q, second_q):
        pair = (first_q, second_q)
        pages = [listed(0, ahead(q) + k * n, slots - 1) for q in pair for k in range(2)]
        ends = [limits[pl.ds(ahead(q), 1), :] for q in pair]
        maxima, totals, sums = column_sums(
            jnp.concatenate([q_in[q] for q in pair], axis=0),
            [kv[at] for at in pages], [vv[at] for at in pages], jnp.where(own_lane < 2, ends[0], ends[1]),
        )
        largest = jnp.maximum(jnp.max(jnp.abs(sums), axis=1, keepdims=True), 1e-30)
        coded = jnp.round(sums * (TOP / largest)).astype(I32).astype(jnp.int16)
        largest_row = jnp.sum(jnp.where(square_1, largest, 0.0), axis=0, keepdims=True)
        stats = stat_pair(maxima + jnp.log(totals), largest_row / (TOP * totals))
        for at, q in enumerate(pair):
            sum_out[pl.ds(2 * q, 2)] = coded[at * 2 * rows : (at + 1) * 2 * rows].reshape(2, rows, HD)
            stat_out[q] = stats[at]

    def serve(step, carry):
        qs = [order(step * SERVE + at) for at in range(SERVE)]
        for q in qs:
            q_copy(q).wait_recv()
        for at in range(0, SERVE, 2):
            serve_pair(qs[at], qs[at + 1])
        for q in qs:
            sum_copy(q).start()
            stat_copy(q).start()
        return carry

    whole = (n - 2) // SERVE
    lax.fori_loop(0, whole, serve, 0)
    rest = [order(step) for step in range(whole * SERVE, n - 1)]
    for q in rest:
        q_copy(q).wait_recv()
    for at in range(0, len(rest), 2):
        serve_pair(rest[at], rest[at + 1] if at + 1 < len(rest) else 0)
    for q in rest:
        sum_copy(q).start()
        stat_copy(q).start()

    def wait_sums(buffer, sem):
        view = buffer.at[pl.ds(2, 2 * n - 2)]
        pltpu.make_async_copy(view, view, sem).wait()

    wait_sums(sum_in, sum_recv)
    wait_all(stat_in, stat_recv, n - 1)

    short = (rows, HD)
    skew = iota(short, 1) - iota(short, 0)

    def combine(i, carry):
        means, logs = [], []
        for p in range(2):
            origin = listed(2, p * requests + i, 2 * n)
            away = jnp.maximum(origin - 1, 0)
            moved = origin > 0
            stats = jnp.where(moved, stat_in[lax.div(away, 2)], near_stat[i])
            skip = jnp.where(moved, lax.rem(away, 2), p) * rows
            logs.append(jnp.sum(jnp.where(skew == skip, stats, 0.0), axis=1, keepdims=True))
            factor = jnp.sum(jnp.where(skew == skip + 2 * rows, stats, 0.0), axis=1, keepdims=True)
            means.append(jnp.where(moved, sum_in[away].astype(F32), near[i, pl.ds(p * rows, rows)]) * factor)
        at = pl.ds(pl.multiple_of(i * rows, rows), rows)
        means.append(draft[at, :])
        logs.append(draft_log[at, :])
        largest = jnp.maximum(jnp.maximum(logs[0], logs[1]), logs[2])
        factors = [jnp.exp(log - largest) for log in logs]
        numerator = factors[0] * means[0] + factors[1] * means[1] + factors[2] * means[2]
        result = numerator / (factors[0] + factors[1] + factors[2])
        attention[at, :] = result
        squares[i] = jnp.sum((result * result).reshape(steps, heads, HD), axis=1)
        return carry

    lax.fori_loop(0, requests, combine, 0, unroll=COMBINE)

    tokens = requests * steps
    total_c = jnp.sum(squares[...].reshape(tokens, HD), axis=1, keepdims=True)
    norm_rows[0] = to_row(total_c, tokens)

    def norm_copy(other):
        return pltpu.make_async_remote_copy(
            src_ref=norm_rows.at[0], dst_ref=norm_rows.at[other], send_sem=norm_send.at[other], recv_sem=norm_recv.at[other],
            device_id=(me, lax.rem(lane_me + other, tp)), device_id_type=MESH,
        )

    for other in range(1, tp):
        norm_copy(other).start()
    for other in range(1, tp):
        norm_copy(other).wait_recv()
    total = norm_rows[0]
    for other in range(1, tp):
        total = total + norm_rows[other]
    scale = lax.rsqrt(total * (1.0 / (tp * width)) + 1e-05)
    scales[...] = jnp.broadcast_to(to_column(scale, tokens), (tokens, HD)).reshape(requests, steps, HD)

    def finish(i, carry):
        for h in range(heads):
            at = slice(h * HD, (h + 1) * HD)
            out_ref[i, :, at] = attention[pl.ds(i * rows + h, steps, stride=heads), :] * scales[i] * gain_ref[:, at]
        return carry

    lax.fori_loop(0, requests, finish, 0)

    for other in range(1, tp):
        norm_copy(other).wait_send()
    for other in range(1, nz):
        row_copy(other, mz).wait_send()
    for other in range(1, ny):
        column_copy(other, my).wait_send()
    wait_all(q_out, q_send, n - 1)
    wait_sums(sum_out, sum_send)
    wait_all(stat_out, stat_send, n - 1)


def per_device(n, nz, tp, queries, new_keys, new_values, key_pool, value_pool, block_table, context, source, replica, target, gain):
    requests, steps, width = queries.shape
    rows = steps * width // HD
    slots, page, _ = key_pool.shape
    entries = source.shape[0]
    vmem = pl.BlockSpec(memory_space=pltpu.VMEM)
    anywhere = pl.BlockSpec(memory_space=pl.ANY)
    dma = pltpu.SemaphoreType.DMA
    table = block_table.T
    return pl.pallas_call(
        functools.partial(kernel, n, nz, tp),
        out_shape=jax.ShapeDtypeStruct((requests, steps, width), F32),
        in_specs=[anywhere] * 11,
        out_specs=vmem,
        scratch_shapes=[
            pltpu.SMEM((2, requests), I32),
            pltpu.SMEM((1, requests), I32),
            pltpu.VMEM((requests, steps, width), BF16),
            pltpu.VMEM((requests, steps, HD), BF16),
            pltpu.VMEM((requests, steps, HD), BF16),
            pltpu.VMEM((2, requests), I32),
            pltpu.VMEM((1, requests), I32),
            pltpu.VMEM((1, entries), I32),
            pltpu.VMEM((1, entries), I32),
            pltpu.VMEM((1, entries), I32),
            pltpu.VMEM((1, width), F32),
            pltpu.VMEM((slots, page, HD), BF16),
            pltpu.VMEM((slots, page, HD), BF16),
            pltpu.VMEM(((requests + 1) * rows, HD), F32),
            pltpu.VMEM((requests, rows, HD), BF16),
            pltpu.VMEM((requests * steps, HD), F32),
            pltpu.VMEM((requests * steps, HD), F32),
            pltpu.VMEM((n // nz, nz, 2, HD), I32),
            pltpu.VMEM((8, HD), I32),
            pltpu.SMEM((8, HD), I32),
            pltpu.VMEM((n + 8, slots), F32),
            pltpu.VMEM((n, 2 * rows, HD), BF16),
            pltpu.VMEM((n, 2 * rows, HD), BF16),
            pltpu.VMEM((2 * n, rows, HD), jnp.int16),
            pltpu.VMEM((2 * n, rows, HD), jnp.int16),
            pltpu.VMEM((n, 1, HD), F32),
            pltpu.VMEM((n, 1, HD), F32),
            pltpu.VMEM((requests, 2 * rows, HD), F32),
            pltpu.VMEM((requests, 1, HD), F32),
            pltpu.VMEM((requests * rows, HD), F32),
            pltpu.VMEM((requests * rows, HD), F32),
            pltpu.VMEM(((requests + 1) * rows, HD), F32),
            pltpu.VMEM((requests, steps, HD), F32),
            pltpu.VMEM((requests, steps, HD), F32),
            pltpu.VMEM((tp, 1, HD), F32),
            dma((13,)), dma, dma((nz,)), dma((nz,)), dma((n // nz,)), dma((n // nz,)), dma, dma((n,)), dma, dma, dma, dma, dma((tp,)), dma((tp,)),
        ],
        compiler_params=pltpu.CompilerParams(collective_id=0, has_side_effects=True, vmem_limit_bytes=40 * 2**20),
    )(
        queries, new_keys, new_values, key_pool, value_pool, table,
        context.reshape(1, requests), source.reshape(1, entries), replica.reshape(1, entries), target.reshape(1, entries),
        gain.reshape(1, width),
    )


def solution(mesh):
    n, tp = mesh.shape["rep"], mesh.shape["tp"]
    nz = 2 ** (n.bit_length() // 2)
    heads, replicas = P("rep", None, "tp"), P("rep")
    return jax.shard_map(
        functools.partial(per_device, n, nz, tp),
        mesh=mesh,
        in_specs=(heads, heads, heads, heads, heads, P("rep", None), replicas, replicas, replicas, replicas, P("tp")),
        out_specs=heads,
        check_vma=False,
    )
```

```python
import functools
import math

import jax
import jax.numpy as jnp
from jax import lax
from jax.experimental import pallas as pl
from jax.experimental.pallas import tpu as pltpu
from jax.sharding import PartitionSpec as P

HD = 128
MASKED = -1e30
HUGE = 3e38
TOP = 32767.0
OWN = 4
SERVE = 4
SKIPS = 1
COMBINE = 4
STRIDE = 27
MESH = pl.DeviceIdType.MESH
I32 = jnp.int32
F32 = jnp.float32
BF16 = jnp.bfloat16


def iota(shape, dim):
    return lax.broadcasted_iota(I32, shape, dim)


def to_column(row, size):
    shape = (size, size)
    return jnp.sum(jnp.where(iota(shape, 0) == iota(shape, 1), row, 0.0), axis=1, keepdims=True)


def to_row(column, size):
    shape = (size, size)
    return jnp.sum(jnp.where(iota(shape, 0) == iota(shape, 1), column, 0.0), axis=0, keepdims=True)


def column_sums(queries, keys, values, limit):
    page = keys[0].shape[0]
    rows = HD // len(keys)
    shape = (page, HD)
    slot = iota(shape, 1) // rows
    products = [
        lax.dot_general(key, queries, (((1,), (1,)), ((), ())), preferred_element_type=F32) for key in keys
    ]
    scores = products[0]
    for b in range(1, len(keys)):
        scores = jnp.where(slot == b, products[b], scores)
    scores = jnp.where(iota(shape, 0).astype(F32) < limit, scores * (1.0 / math.sqrt(HD)), MASKED)
    maxima = jnp.max(scores, axis=0, keepdims=True)
    weights = jnp.exp(scores - maxima)
    totals = jnp.sum(weights, axis=0, keepdims=True)
    turned = weights.T.astype(BF16)
    sums = [
        jnp.dot(turned[b * rows : (b + 1) * rows], values[b], preferred_element_type=F32) for b in range(len(keys))
    ]
    return maxima, totals, jnp.concatenate(sums, axis=0)


def block_sums(queries, keys, values, caps):
    scores = lax.dot_general(queries, keys, (((1,), (1,)), ((), ())), preferred_element_type=F32)
    scores = jnp.minimum(scores * (1.0 / math.sqrt(HD)), caps)
    maxima = jnp.max(scores, axis=1, keepdims=True)
    weights = jnp.exp(scores - maxima)
    totals = jnp.sum(weights, axis=1, keepdims=True)
    sums = jnp.dot(weights.astype(BF16), values, preferred_element_type=F32)
    return maxima, totals, sums


def reach(n, nz):
    ny = n // nz
    near = [q for q in range(1, n) if hops(q, ny, nz) <= (2 if n > 16 else 1)]
    far, q = [], 0
    while len(far) < n - 1 - len(near):
        q = (q + STRIDE) % n
        if q and q not in near:
            far.append(q)
    return near, far


def hops(q, ny, nz):
    y, z = q // nz, q % nz
    return min(y, ny - y) + min(z, nz - z)


def kernel(
    n, nz, tp,
    q_hbm, nk_hbm, nv_hbm, kp_ref, vp_ref, table_hbm, context_hbm, source_hbm, replica_hbm, target_hbm, gain_hbm,
    out_ref,
    table_s, context_s, q_ref, nk_ref, nv_ref, table_ref, context_ref, source_ref, replica_ref, target_ref, gain_ref,
    kv, vv, qf, qb, nk, nv,
    near_out, near_in, note_out, note_in, lists, lists_s, sources, sources_s, limits,
    q_out, q_in, sum_out, sum_in, stat_out, stat_in,
    near, near_stat, draft, draft_log, attention, squares, scales, norm_rows,
    in_sem, list_sem, near_send, near_recv, note_send, note_recv, q_send, q_recv, sum_send, sum_recv, stat_send, stat_recv, norm_send, norm_recv,
):
    ny = n // nz
    requests, steps, width = q_hbm.shape
    heads = width // HD
    rows = steps * heads
    entries = replica_hbm.shape[1]
    slots = kp_ref.shape[0]
    page = kp_ref.shape[1]
    me = lax.axis_index("rep")
    lane_me = lax.axis_index("tp")
    my, mz = lax.div(me, nz), lax.rem(me, nz)

    def ahead(q):
        return lax.rem(my + lax.div(q, nz), ny) * nz + lax.rem(mz + lax.rem(q, nz), nz)

    def behind(q):
        return lax.rem(my + ny - lax.div(q, nz), ny) * nz + lax.rem(mz + nz - lax.rem(q, nz), nz)

    def opposite(q):
        return lax.rem(ny - lax.div(q, nz), ny) * nz + lax.rem(nz - lax.rem(q, nz), nz)

    def order(step):
        return lax.rem((step + 1) * STRIDE, n)

    near_q, far_q = reach(n, nz)
    far = len(far_q)

    def following(q):
        for turn in range(SKIPS + 1):
            there = lax.rem(q + STRIDE, n)
            if turn > 0:
                y, z = lax.div(q, nz), lax.rem(q, nz)
                away = jnp.minimum(y, ny - y) + jnp.minimum(z, nz - z)
                there = jnp.where(away <= (2 if n > 16 else 1), there, q)
            q = there
        return q

    moves = [
        (replica_hbm, replica_ref), (source_hbm, source_ref), (target_hbm, target_ref), (table_hbm, table_ref),
        (context_hbm, context_ref), (q_hbm, q_ref), (table_hbm, table_s), (context_hbm, context_s), (nk_hbm, nk_ref),
        (nv_hbm, nv_ref), (kp_ref, kv), (vp_ref, vv), (gain_hbm, gain_ref),
    ]
    fetches = [pltpu.make_async_copy(a, b, in_sem.at[at]) for at, (a, b) in enumerate(moves)]
    for fetch in fetches:
        fetch.start()

    barrier = pltpu.get_barrier_semaphore()

    def greet(step, carry):
        pl.semaphore_signal(barrier, inc=1, device_id=(ahead(step + 1), lane_me), device_id_type=MESH)
        return carry

    lax.fori_loop(0, n - 1, greet, 0)
    for other in range(1, tp):
        pl.semaphore_signal(barrier, inc=1, device_id=(me, lax.rem(lane_me + other, tp)), device_id_type=MESH)

    for fetch in fetches[0:5]:
        fetch.wait()

    replica = replica_ref[...].astype(F32)
    source = source_ref[...].astype(F32)
    target = target_ref[...].astype(F32)
    square = (entries, entries)
    replica_c = to_column(replica, entries)
    same_before = (replica_c == replica) & (iota(square, 0) < iota(square, 1))
    rank = jnp.sum(jnp.where(same_before, 1.0, 0.0), axis=0, keepdims=True)
    rank_c = to_column(rank, entries)
    source_c = to_column(source, entries)

    def vector_peer(q, sign):
        dy, dz = q // nz, q % nz
        return (((my + ny + sign * dy) % ny) * nz + (mz + nz + sign * dz) % nz).astype(F32)

    def targets_of(sign):
        peers = vector_peer(iota((n, entries), 0), sign)
        found = []
        for k in range(2):
            chosen = (peers == replica) & (rank == float(k))
            found.append(jnp.sum(jnp.where(chosen, target + 1.0, 0.0), axis=1, keepdims=True) - 1.0)
        return found

    wide = (entries, 2 * n)
    peers_row = vector_peer(iota(wide, 1) % n, 1)
    chosen = (replica_c == peers_row) & (rank_c == (iota(wide, 1) // n).astype(F32))
    source_row = jnp.sum(jnp.where(chosen, source_c, 0.0), axis=0, keepdims=True)

    sources[...] = jnp.zeros(sources.shape, I32)
    sources[0:1, 0 : 2 * n] = source_row.astype(I32)
    source_copy = pltpu.make_async_copy(sources, sources_s, list_sem)
    source_copy.start()

    context_c = to_column(context_ref[...].astype(F32), requests)
    by_slot = (requests, slots)
    slot_lane = iota(by_slot, 1).astype(F32)
    request_c = iota(by_slot, 0).astype(F32)
    valid_row = jnp.zeros((1, slots), F32)
    place_row = jnp.zeros((1, slots), F32)
    for p in range(2):
        table_c = to_column(table_ref[p : p + 1, :].astype(F32), requests)
        here = table_c == slot_lane
        valid = jnp.clip(context_c - float(p * page), 0.0, float(page))
        valid_row += jnp.sum(jnp.where(here, valid, 0.0), axis=0, keepdims=True)
        place_row += jnp.sum(jnp.where(here, request_c + float(p * requests), 0.0), axis=0, keepdims=True)

    notes = (n, slots)
    lane = iota(notes, 1).astype(F32)
    first, second = targets_of(1)
    marks = jnp.where(lane == first, 65536.0, 0.0) + jnp.where(lane == second, 131072.0, 0.0)
    code = (valid_row + marks).astype(I32)
    for q in range(n):
        note_out[q] = code[q : q + 1, :]
    first_back, second_back = targets_of(-1)
    note_in[0] = jnp.zeros((1, slots), I32)
    q_at = iota((n, HD), 0)
    far_number = jnp.zeros((n, HD), F32)
    near_number = jnp.zeros((n, HD), F32)
    for at, q in enumerate(far_q):
        far_number = jnp.where(q_at == q, at + 1.0, far_number)
    for at, q in enumerate(near_q):
        near_number = jnp.where(q_at == q, at + 1.0, near_number)

    for fetch in fetches[6:]:
        fetch.wait()
    source_copy.wait()
    for at, q in enumerate(near_q):
        for k in range(2):
            page_at = jnp.minimum(jnp.maximum(sources_s[0, q + k * n], 0), slots - 1)
            near_out[2 * at + k, 0] = kv[page_at]
            near_out[2 * at + k, 1] = vv[page_at]

    pl.semaphore_wait(barrier, n - 1 + tp - 1)

    def note_copy(q):
        return pltpu.make_async_remote_copy(
            src_ref=note_out.at[q], dst_ref=note_in.at[q], send_sem=note_send, recv_sem=note_recv,
            device_id=(ahead(q), lane_me), device_id_type=MESH,
        )

    def send_note(step, carry):
        note_copy(order(step)).start()
        return carry

    lax.fori_loop(0, n - 1, send_note, 0)

    def near_copy(at):
        return pltpu.make_async_remote_copy(
            src_ref=near_out.at[pl.ds(2 * at, 2)], dst_ref=near_in.at[pl.ds(2 * at, 2)], send_sem=near_send.at[at],
            recv_sem=near_recv.at[at], device_id=(ahead(near_q[at]), lane_me), device_id_type=MESH,
        )

    for at in range(len(near_q)):
        near_copy(at).start()

    fetches[5].wait()

    def spread(i, carry):
        for h in range(heads):
            qf[pl.ds(i * rows + h, steps, stride=heads), :] = q_ref[i, :, h * HD : (h + 1) * HD].astype(F32)
        return carry

    lax.fori_loop(0, requests, spread, 0)

    def narrow(i, carry):
        qb[i] = qf[pl.ds(pl.multiple_of(i * rows, rows), rows), :].astype(BF16)
        return carry

    lax.fori_loop(0, requests, narrow, 0)

    def wait_all(buffer, sem, start, count):
        view = buffer.at[pl.ds(start, count)]
        pltpu.make_async_copy(view, view, sem).wait()

    wait_all(note_in, note_recv, 1, n - 1)

    got = note_in[...].reshape(n, slots)
    mark = got >> 16
    count = (got & 65535).astype(F32)
    place_0 = jnp.sum(jnp.where(mark == 1, place_row + 1.0, 0.0), axis=1, keepdims=True) - 1.0
    place_1 = jnp.sum(jnp.where(mark == 2, place_row + 1.0, 0.0), axis=1, keepdims=True) - 1.0
    valid_0 = jnp.sum(jnp.where(lane == first_back, count, 0.0), axis=1, keepdims=True)
    valid_1 = jnp.sum(jnp.where(lane == second_back, count, 0.0), axis=1, keepdims=True)
    half = lane - jnp.where(lane >= float(2 * rows), float(2 * rows), 0.0)
    limits[0:n] = jnp.where(half < float(rows), valid_0, valid_1)

    line = (n, 2 * n)
    lane_2 = iota(line, 1)
    distance = iota(line, 0)
    request_0 = jnp.maximum(place_0, 0.0) - jnp.where(place_0 >= float(requests), float(requests), 0.0)
    request_1 = jnp.maximum(place_1, 0.0) - jnp.where(place_1 >= float(requests), float(requests), 0.0)
    request_row = jnp.sum(
        jnp.where(lane_2 == distance, request_0, 0.0) + jnp.where(lane_2 == distance + n, request_1, 0.0),
        axis=0, keepdims=True,
    )
    place_lane = iota((n, HD), 1).astype(F32)

    def origins(number):
        mine = jnp.where(place_lane == place_0, 1.0, 0.0) + jnp.where(place_lane == place_1, 2.0, 0.0)
        return jnp.sum(jnp.where((mine > 0.0) & (number > 0.0), 2.0 * number - 2.0 + mine, 0.0), axis=0, keepdims=True)

    lists[...] = jnp.zeros(lists.shape, I32)
    lists[0:1, 0:HD] = origins(near_number).astype(I32)
    lists[1:2, 0 : 2 * n] = request_row.astype(I32)
    lists[2:3, :] = origins(far_number).astype(I32)
    list_copy = pltpu.make_async_copy(lists, lists_s, list_sem)
    list_copy.start()
    list_copy.wait()

    def listed(line, at, limit):
        return jnp.minimum(jnp.maximum(lists_s[line, at], 0), limit)

    def q_copy(at, q):
        return pltpu.make_async_remote_copy(
            src_ref=q_out.at[at], dst_ref=q_in.at[at], send_sem=q_send, recv_sem=q_recv.at[at],
            device_id=(behind(q), lane_me), device_id_type=MESH,
        )

    def send_queries(at, q):
        q_out[at, 0:rows] = qb[listed(1, q, requests - 1)]
        q_out[at, rows : 2 * rows] = qb[listed(1, q + n, requests - 1)]
        q_copy(at, q).start()
        return following(q)

    lax.fori_loop(0, far, send_queries, far_q[0])

    for at in range(len(near_q)):
        near_copy(at).wait_recv()
    lane_1 = iota((1, HD), 1)
    own_lane = lane_1 // rows

    def stat_pair(logs, factors):
        low = lane_1 < 2 * rows
        return (
            jnp.where(low, logs, pltpu.roll(factors, 2 * rows, axis=1)),
            jnp.where(low, pltpu.roll(logs, 2 * rows, axis=1), factors),
        )

    def own_pages(step, carry):
        pair = (2 * step, 2 * step + 1)
        first_context, second_context = context_s[0, pair[0]], context_s[0, pair[1]]
        limit = jnp.where(own_lane < 2, first_context, second_context) - jnp.where(own_lane % 2 == 1, page, 0)
        keys, values = [], []
        for i in pair:
            for p in range(2):
                arrived = listed(0, p * requests + i, 2 * len(near_q))
                landed = jnp.maximum(arrived - 1, 0)
                at = table_s[p, i]
                keys.append(jnp.where(arrived > 0, near_in[landed, 0], kv[at]))
                values.append(jnp.where(arrived > 0, near_in[landed, 1], vv[at]))
        mine = [qb[i] for i in pair]
        maxima, totals, sums = column_sums(
            jnp.concatenate([mine[0], mine[0], mine[1], mine[1]], axis=0),
            keys, values, limit.astype(F32),
        )
        stats = stat_pair(maxima + jnp.log(totals), 1.0 / totals)
        for at, i in enumerate(pair):
            near[i] = sums[at * 2 * rows : (at + 1) * 2 * rows]
            near_stat[i] = stats[at]
        return carry

    lax.fori_loop(0, requests // 2, own_pages, 0, unroll=OWN)

    for i in range(requests):
        nk[i * steps : (i + 1) * steps, :] = nk_ref[i].astype(F32)
        nv[i * steps : (i + 1) * steps, :] = nv_ref[i].astype(F32)
    draft_keys = nk[...].astype(BF16)
    draft_values = nv[...].astype(BF16)
    chunk = HD // rows
    blocky = (HD, HD)
    key_at = iota(blocky, 1)
    row_at = iota(blocky, 0)

    def own_draft(c, carry):
        request = c * chunk + row_at // rows
        allowed = (key_at // steps == request) & (key_at % steps <= (row_at % rows) // heads)
        block = qb[pl.ds(c * chunk, chunk)].reshape(HD, HD)
        maxima, totals, sums = block_sums(block, draft_keys, draft_values, jnp.where(allowed, HUGE, MASKED))
        at = pl.ds(pl.multiple_of(c * HD, HD), HD)
        draft[at, :] = sums / totals
        draft_log[at, :] = jnp.broadcast_to(maxima + jnp.log(totals), blocky)
        return carry

    lax.fori_loop(0, requests // chunk, own_draft, 0, unroll=2)

    def sum_copy(at, q):
        return pltpu.make_async_remote_copy(
            src_ref=sum_out.at[pl.ds(2 * at, 2)], dst_ref=sum_in.at[pl.ds(2 * at, 2)], send_sem=sum_send, recv_sem=sum_recv,
            device_id=(ahead(q), lane_me), device_id_type=MESH,
        )

    def stat_copy(at, q):
        return pltpu.make_async_remote_copy(
            src_ref=stat_out.at[at], dst_ref=stat_in.at[at], send_sem=stat_send, recv_sem=stat_recv,
            device_id=(ahead(q), lane_me), device_id_type=MESH,
        )

    square_1 = iota(blocky, 0) == iota(blocky, 1)

    def serve_pair(start, pair):
        pages = [jnp.minimum(jnp.maximum(sources_s[0, q + k * n], 0), slots - 1) for q in pair for k in range(2)]
        ends = [limits[pl.ds(opposite(q), 1), :] for q in pair]
        maxima, totals, sums = column_sums(
            jnp.concatenate([q_in[start], q_in[start + 1]], axis=0),
            [kv[at] for at in pages], [vv[at] for at in pages], jnp.where(own_lane < 2, ends[0], ends[1]),
        )
        largest = jnp.maximum(jnp.max(jnp.abs(sums), axis=1, keepdims=True), 1e-30)
        coded = jnp.round(sums * (TOP / largest)).astype(I32).astype(jnp.int16)
        largest_row = jnp.sum(jnp.where(square_1, largest, 0.0), axis=0, keepdims=True)
        stats = stat_pair(maxima + jnp.log(totals), largest_row / (TOP * totals))
        for k in range(2):
            sum_out[pl.ds(2 * (start + k), 2)] = coded[k * 2 * rows : (k + 1) * 2 * rows].reshape(2, rows, HD)
            stat_out[start + k] = stats[k]

    def serve_some(start, qs):
        for at, q in enumerate(qs):
            q_copy(start + at, q).wait_recv()
        for at in range(0, len(qs), 2):
            serve_pair(start + at, (qs[at], qs[at + 1] if at + 1 < len(qs) else 0))
        for at, q in enumerate(qs):
            sum_copy(start + at, q).start()
            stat_copy(start + at, q).start()

    def serve(step, q):
        qs = [q]
        for _ in range(SERVE):
            qs.append(following(qs[-1]))
        serve_some(step * SERVE, qs[:-1])
        return qs[-1]

    q_in[far] = jnp.zeros((2 * rows, HD), BF16)
    whole = (far - 1) // SERVE
    lax.fori_loop(0, whole, serve, far_q[0])
    serve_some(whole * SERVE, far_q[whole * SERVE :])

    wait_all(sum_in, sum_recv, 0, 2 * far)
    wait_all(stat_in, stat_recv, 0, far)

    short = (rows, HD)
    skew = iota(short, 1) - iota(short, 0)

    def combine(i, carry):
        means, logs = [], []
        for p in range(2):
            origin = listed(2, p * requests + i, 2 * far)
            away = jnp.maximum(origin - 1, 0)
            moved = origin > 0
            stats = jnp.where(moved, stat_in[lax.div(away, 2)], near_stat[i])
            skip = jnp.where(moved, lax.rem(away, 2), p) * rows
            logs.append(jnp.sum(jnp.where(skew == skip, stats, 0.0), axis=1, keepdims=True))
            factor = jnp.sum(jnp.where(skew == skip + 2 * rows, stats, 0.0), axis=1, keepdims=True)
            means.append(jnp.where(moved, sum_in[away].astype(F32), near[i, pl.ds(p * rows, rows)]) * factor)
        at = pl.ds(pl.multiple_of(i * rows, rows), rows)
        means.append(draft[at, :])
        logs.append(draft_log[at, :])
        largest = jnp.maximum(jnp.maximum(logs[0], logs[1]), logs[2])
        factors = [jnp.exp(log - largest) for log in logs]
        numerator = factors[0] * means[0] + factors[1] * means[1] + factors[2] * means[2]
        result = numerator / (factors[0] + factors[1] + factors[2])
        attention[at, :] = result
        squares[i] = jnp.sum((result * result).reshape(steps, heads, HD), axis=1)
        return carry

    lax.fori_loop(0, requests, combine, 0, unroll=COMBINE)

    tokens = requests * steps
    total_c = jnp.sum(squares[...].reshape(tokens, HD), axis=1, keepdims=True)
    norm_rows[0] = to_row(total_c, tokens)

    def norm_copy(other):
        return pltpu.make_async_remote_copy(
            src_ref=norm_rows.at[0], dst_ref=norm_rows.at[other], send_sem=norm_send.at[other], recv_sem=norm_recv.at[other],
            device_id=(me, lax.rem(lane_me + other, tp)), device_id_type=MESH,
        )

    for other in range(1, tp):
        norm_copy(other).start()
    for other in range(1, tp):
        norm_copy(other).wait_recv()
    total = norm_rows[0]
    for other in range(1, tp):
        total = total + norm_rows[other]
    scale = lax.rsqrt(total * (1.0 / (tp * width)) + 1e-05)
    scales[...] = jnp.broadcast_to(to_column(scale, tokens), (tokens, HD)).reshape(requests, steps, HD)

    def finish(i, carry):
        for h in range(heads):
            at = slice(h * HD, (h + 1) * HD)
            out_ref[i, :, at] = attention[pl.ds(i * rows + h, steps, stride=heads), :] * scales[i] * gain_ref[:, at]
        return carry

    lax.fori_loop(0, requests, finish, 0)

    for other in range(1, tp):
        norm_copy(other).wait_send()
    for at in range(len(near_q)):
        near_copy(at).wait_send()
    wait_all(note_out, note_send, 1, n - 1)
    wait_all(q_out, q_send, 0, far)
    wait_all(sum_out, sum_send, 0, 2 * far)
    wait_all(stat_out, stat_send, 0, far)


def per_device(n, nz, tp, queries, new_keys, new_values, key_pool, value_pool, block_table, context, source, replica, target, gain):
    requests, steps, width = queries.shape
    rows = steps * width // HD
    slots, page, _ = key_pool.shape
    entries = source.shape[0]
    vmem = pl.BlockSpec(memory_space=pltpu.VMEM)
    anywhere = pl.BlockSpec(memory_space=pl.ANY)
    dma = pltpu.SemaphoreType.DMA
    table = block_table.T
    near, far = (len(distances) for distances in reach(n, nz))
    return pl.pallas_call(
        functools.partial(kernel, n, nz, tp),
        out_shape=jax.ShapeDtypeStruct((requests, steps, width), F32),
        in_specs=[anywhere] * 11,
        out_specs=vmem,
        scratch_shapes=[
            pltpu.SMEM((2, requests), I32),
            pltpu.SMEM((1, requests), I32),
            pltpu.VMEM((requests, steps, width), BF16),
            pltpu.VMEM((requests, steps, HD), BF16),
            pltpu.VMEM((requests, steps, HD), BF16),
            pltpu.VMEM((2, requests), I32),
            pltpu.VMEM((1, requests), I32),
            pltpu.VMEM((1, entries), I32),
            pltpu.VMEM((1, entries), I32),
            pltpu.VMEM((1, entries), I32),
            pltpu.VMEM((1, width), F32),
            pltpu.VMEM((slots, page, HD), BF16),
            pltpu.VMEM((slots, page, HD), BF16),
            pltpu.VMEM(((requests + 1) * rows, HD), F32),
            pltpu.VMEM((requests, rows, HD), BF16),
            pltpu.VMEM((requests * steps, HD), F32),
            pltpu.VMEM((requests * steps, HD), F32),
            pltpu.VMEM((2 * near, 2, page, HD), BF16),
            pltpu.VMEM((2 * near, 2, page, HD), BF16),
            pltpu.VMEM((n, 1, slots), I32),
            pltpu.VMEM((n, 1, slots), I32),
            pltpu.VMEM((8, HD), I32),
            pltpu.SMEM((8, HD), I32),
            pltpu.VMEM((8, HD), I32),
            pltpu.SMEM((8, HD), I32),
            pltpu.VMEM((n + 8, slots), F32),
            pltpu.VMEM((far + 1, 2 * rows, HD), BF16),
            pltpu.VMEM((far + 1, 2 * rows, HD), BF16),
            pltpu.VMEM((2 * far + 2, rows, HD), jnp.int16),
            pltpu.VMEM((2 * far + 2, rows, HD), jnp.int16),
            pltpu.VMEM((far + 1, 1, HD), F32),
            pltpu.VMEM((far + 1, 1, HD), F32),
            pltpu.VMEM((requests, 2 * rows, HD), F32),
            pltpu.VMEM((requests, 1, HD), F32),
            pltpu.VMEM((requests * rows, HD), F32),
            pltpu.VMEM((requests * rows, HD), F32),
            pltpu.VMEM(((requests + 1) * rows, HD), F32),
            pltpu.VMEM((requests, steps, HD), F32),
            pltpu.VMEM((requests, steps, HD), F32),
            pltpu.VMEM((tp, 1, HD), F32),
            dma((13,)), dma, dma((near,)), dma((near,)), dma, dma, dma, dma((far,)), dma, dma, dma, dma, dma((tp,)), dma((tp,)),
        ],
        compiler_params=pltpu.CompilerParams(collective_id=0, has_side_effects=True, vmem_limit_bytes=56 * 2**20),
    )(
        queries, new_keys, new_values, key_pool, value_pool, table,
        context.reshape(1, requests), source.reshape(1, entries), replica.reshape(1, entries), target.reshape(1, entries),
        gain.reshape(1, width),
    )


def solution(mesh):
    n, tp = mesh.shape["rep"], mesh.shape["tp"]
    nz = 2 ** (n.bit_length() // 2)
    heads, replicas = P("rep", None, "tp"), P("rep")
    return jax.shard_map(
        functools.partial(per_device, n, nz, tp),
        mesh=mesh,
        in_specs=(heads, heads, heads, heads, heads, P("rep", None), replicas, replicas, replicas, replicas, P("tp")),
        out_specs=heads,
        check_vma=False,
    )
```

```python
import functools
import math

import jax
import jax.numpy as jnp
from jax import lax
from jax.experimental import pallas as pl
from jax.experimental.pallas import tpu as pltpu
from jax.sharding import PartitionSpec as P

HD = 128
MASKED = -1e30
HUGE = 3e38
TOP = 32767.0
OWN = 4
SERVE = 4
COMBINE = 4
STRIDE = 27
MESH = pl.DeviceIdType.MESH
I32 = jnp.int32
F32 = jnp.float32
BF16 = jnp.bfloat16


def iota(shape, dim):
    return lax.broadcasted_iota(I32, shape, dim)


def to_column(row, size):
    shape = (size, size)
    return jnp.sum(jnp.where(iota(shape, 0) == iota(shape, 1), row, 0.0), axis=1, keepdims=True)


def to_row(column, size):
    shape = (size, size)
    return jnp.sum(jnp.where(iota(shape, 0) == iota(shape, 1), column, 0.0), axis=0, keepdims=True)


def column_sums(queries, keys, values, limit):
    page = keys[0].shape[0]
    rows = HD // len(keys)
    shape = (page, HD)
    slot = iota(shape, 1) // rows
    products = [
        lax.dot_general(key, queries, (((1,), (1,)), ((), ())), preferred_element_type=F32) for key in keys
    ]
    scores = products[0]
    for b in range(1, len(keys)):
        scores = jnp.where(slot == b, products[b], scores)
    scores = jnp.where(iota(shape, 0).astype(F32) < limit, scores * (1.0 / math.sqrt(HD)), MASKED)
    maxima = jnp.max(scores, axis=0, keepdims=True)
    weights = jnp.exp(scores - maxima)
    totals = jnp.sum(weights, axis=0, keepdims=True)
    turned = weights.T.astype(BF16)
    sums = [
        jnp.dot(turned[b * rows : (b + 1) * rows], values[b], preferred_element_type=F32) for b in range(len(keys))
    ]
    return maxima, totals, jnp.concatenate(sums, axis=0)


def block_sums(queries, keys, values, caps):
    scores = lax.dot_general(queries, keys, (((1,), (1,)), ((), ())), preferred_element_type=F32)
    scores = jnp.minimum(scores * (1.0 / math.sqrt(HD)), caps)
    maxima = jnp.max(scores, axis=1, keepdims=True)
    weights = jnp.exp(scores - maxima)
    totals = jnp.sum(weights, axis=1, keepdims=True)
    sums = jnp.dot(weights.astype(BF16), values, preferred_element_type=F32)
    return maxima, totals, sums


def reach(n, nz):
    ny = n // nz
    near = [q for q in range(1, n) if hops(q, ny, nz) <= (2 if n > 16 else 1)]
    far, q = [], 0
    while len(far) < n - 1 - len(near):
        q = (q + STRIDE) % n
        if q and q not in near:
            far.append(q)
    return near, far


def hops(q, ny, nz):
    y, z = q // nz, q % nz
    return min(y, ny - y) + min(z, nz - z)


def kernel(
    n, nz, tp,
    q_hbm, nk_hbm, nv_hbm, kp_ref, vp_ref, table_hbm, context_hbm, source_hbm, replica_hbm, target_hbm, gain_hbm,
    out_ref,
    table_s, context_s, q_ref, nk_ref, nv_ref, table_ref, context_ref, source_ref, replica_ref, target_ref, gain_ref,
    kv, vv, qf, qb, nk, nv,
    near_out, near_in, note_out, note_in, lists, lists_s, sources, sources_s, plan_s, limits,
    q_out, q_in, sum_out, sum_in, stat_out, stat_in,
    near, near_stat, draft, draft_log, attention, squares, scales, norm_rows,
    in_sem, list_sem, near_send, near_recv, note_send, note_recv, q_send, q_recv, sum_send, sum_recv, stat_send, stat_recv, norm_send, norm_recv,
):
    ny = n // nz
    requests, steps, width = q_hbm.shape
    heads = width // HD
    rows = steps * heads
    entries = replica_hbm.shape[1]
    slots = kp_ref.shape[0]
    page = kp_ref.shape[1]
    me = lax.axis_index("rep")
    lane_me = lax.axis_index("tp")
    my, mz = lax.div(me, nz), lax.rem(me, nz)

    def ahead(q):
        return lax.rem(my + lax.div(q, nz), ny) * nz + lax.rem(mz + lax.rem(q, nz), nz)

    def behind(q):
        return lax.rem(my + ny - lax.div(q, nz), ny) * nz + lax.rem(mz + nz - lax.rem(q, nz), nz)

    def opposite(q):
        return lax.rem(ny - lax.div(q, nz), ny) * nz + lax.rem(nz - lax.rem(q, nz), nz)

    def order(step):
        return lax.rem((step + 1) * STRIDE, n)

    near_q, far_q = reach(n, nz)
    far = len(far_q)

    barrier = pltpu.get_barrier_semaphore()

    def greet(step, carry):
        pl.semaphore_signal(barrier, inc=1, device_id=(ahead(step + 1), lane_me), device_id_type=MESH)
        return carry

    lax.fori_loop(0, n - 1, greet, 0)
    for other in range(1, tp):
        pl.semaphore_signal(barrier, inc=1, device_id=(me, lax.rem(lane_me + other, tp)), device_id_type=MESH)

    moves = [
        (replica_hbm, replica_ref), (source_hbm, source_ref), (target_hbm, target_ref), (table_hbm, table_ref),
        (context_hbm, context_ref), (q_hbm, q_ref), (table_hbm, table_s), (context_hbm, context_s), (nk_hbm, nk_ref),
        (nv_hbm, nv_ref), (kp_ref, kv), (vp_ref, vv), (gain_hbm, gain_ref),
    ]
    fetches = [pltpu.make_async_copy(a, b, in_sem.at[at]) for at, (a, b) in enumerate(moves)]
    for fetch in fetches:
        fetch.start()

    for at, q in enumerate(far_q):
        plan_s[at] = q
    for fetch in fetches[0:5]:
        fetch.wait()

    replica = replica_ref[...].astype(F32)
    source = source_ref[...].astype(F32)
    target = target_ref[...].astype(F32)
    square = (entries, entries)
    replica_c = to_column(replica, entries)
    same_before = (replica_c == replica) & (iota(square, 0) < iota(square, 1))
    rank = jnp.sum(jnp.where(same_before, 1.0, 0.0), axis=0, keepdims=True)
    rank_c = to_column(rank, entries)
    source_c = to_column(source, entries)

    def vector_peer(q, sign):
        dy, dz = q // nz, q % nz
        return (((my + ny + sign * dy) % ny) * nz + (mz + nz + sign * dz) % nz).astype(F32)

    def targets_of(sign):
        peers = vector_peer(iota((n, entries), 0), sign)
        found = []
        for k in range(2):
            chosen = (peers == replica) & (rank == float(k))
            found.append(jnp.sum(jnp.where(chosen, target + 1.0, 0.0), axis=1, keepdims=True) - 1.0)
        return found

    wide = (entries, 2 * n)
    peers_row = vector_peer(iota(wide, 1) % n, 1)
    chosen = (replica_c == peers_row) & (rank_c == (iota(wide, 1) // n).astype(F32))
    source_row = jnp.sum(jnp.where(chosen, source_c, 0.0), axis=0, keepdims=True)

    sources[...] = jnp.zeros(sources.shape, I32)
    sources[0:1, 0 : 2 * n] = source_row.astype(I32)
    source_copy = pltpu.make_async_copy(sources, sources_s, list_sem)
    source_copy.start()

    context_c = to_column(context_ref[...].astype(F32), requests)
    by_slot = (requests, slots)
    slot_lane = iota(by_slot, 1).astype(F32)
    request_c = iota(by_slot, 0).astype(F32)
    valid_row = jnp.zeros((1, slots), F32)
    place_row = jnp.zeros((1, slots), F32)
    for p in range(2):
        table_c = to_column(table_ref[p : p + 1, :].astype(F32), requests)
        here = table_c == slot_lane
        valid = jnp.clip(context_c - float(p * page), 0.0, float(page))
        valid_row += jnp.sum(jnp.where(here, valid, 0.0), axis=0, keepdims=True)
        place_row += jnp.sum(jnp.where(here, request_c + float(p * requests), 0.0), axis=0, keepdims=True)

    notes = (n, slots)
    lane = iota(notes, 1).astype(F32)
    first, second = targets_of(1)
    marks = jnp.where(lane == first, 65536.0, 0.0) + jnp.where(lane == second, 131072.0, 0.0)
    code = (valid_row + marks).astype(I32)
    for q in range(n):
        note_out[q] = code[q : q + 1, :]
    note_in[0] = jnp.zeros((1, slots), I32)
    pl.semaphore_wait(barrier, n - 1 + tp - 1)

    def note_copy(q):
        return pltpu.make_async_remote_copy(
            src_ref=note_out.at[q], dst_ref=note_in.at[q], send_sem=note_send, recv_sem=note_recv,
            device_id=(ahead(q), lane_me), device_id_type=MESH,
        )

    def send_note(step, carry):
        note_copy(order(step)).start()
        return carry

    lax.fori_loop(0, n - 1, send_note, 0)

    def near_copy(at):
        return pltpu.make_async_remote_copy(
            src_ref=near_out.at[pl.ds(2 * at, 2)], dst_ref=near_in.at[pl.ds(2 * at, 2)], send_sem=near_send.at[at],
            recv_sem=near_recv.at[at], device_id=(ahead(near_q[at]), lane_me), device_id_type=MESH,
        )

    for fetch in fetches[6:]:
        fetch.wait()
    source_copy.wait()
    for at, q in enumerate(near_q):
        for k in range(2):
            page_at = jnp.minimum(jnp.maximum(sources_s[0, q + k * n], 0), slots - 1)
            near_out[2 * at + k, 0] = kv[page_at]
            near_out[2 * at + k, 1] = vv[page_at]

    for at in range(len(near_q)):
        near_copy(at).start()
    first_back, second_back = targets_of(-1)
    q_at = iota((n, HD), 0)
    far_number = jnp.zeros((n, HD), F32)
    near_number = jnp.zeros((n, HD), F32)
    for at, q in enumerate(far_q):
        far_number = jnp.where(q_at == q, at + 1.0, far_number)
    for at, q in enumerate(near_q):
        near_number = jnp.where(q_at == q, at + 1.0, near_number)

    fetches[5].wait()

    def spread(i, carry):
        for h in range(heads):
            qf[pl.ds(i * rows + h, steps, stride=heads), :] = q_ref[i, :, h * HD : (h + 1) * HD].astype(F32)
        return carry

    lax.fori_loop(0, requests, spread, 0)

    def narrow(i, carry):
        qb[i] = qf[pl.ds(pl.multiple_of(i * rows, rows), rows), :].astype(BF16)
        return carry

    lax.fori_loop(0, requests, narrow, 0)

    def wait_all(buffer, sem, start, count):
        view = buffer.at[pl.ds(start, count)]
        pltpu.make_async_copy(view, view, sem).wait()

    wait_all(note_in, note_recv, 1, n - 1)

    got = note_in[...].reshape(n, slots)
    mark = got >> 16
    count = (got & 65535).astype(F32)
    place_0 = jnp.sum(jnp.where(mark == 1, place_row + 1.0, 0.0), axis=1, keepdims=True) - 1.0
    place_1 = jnp.sum(jnp.where(mark == 2, place_row + 1.0, 0.0), axis=1, keepdims=True) - 1.0
    line = (n, 2 * n)
    lane_2 = iota(line, 1)
    distance = iota(line, 0)
    request_0 = jnp.maximum(place_0, 0.0) - jnp.where(place_0 >= float(requests), float(requests), 0.0)
    request_1 = jnp.maximum(place_1, 0.0) - jnp.where(place_1 >= float(requests), float(requests), 0.0)
    request_row = jnp.sum(
        jnp.where(lane_2 == distance, request_0, 0.0) + jnp.where(lane_2 == distance + n, request_1, 0.0),
        axis=0, keepdims=True,
    )
    lists[...] = jnp.zeros(lists.shape, I32)
    lists[1:2, 0 : 2 * n] = request_row.astype(I32)
    list_copy = pltpu.make_async_copy(lists, lists_s, list_sem)
    list_copy.start()
    list_copy.wait()

    def listed(line, at, limit):
        return jnp.minimum(jnp.maximum(lists_s[line, at], 0), limit)

    def q_copy(at, q):
        return pltpu.make_async_remote_copy(
            src_ref=q_out.at[at], dst_ref=q_in.at[at], send_sem=q_send, recv_sem=q_recv.at[at],
            device_id=(behind(q), lane_me), device_id_type=MESH,
        )

    def send_queries(at, carry):
        q = plan_s[at]
        q_out[at, 0:rows] = qb[listed(1, q, requests - 1)]
        q_out[at, rows : 2 * rows] = qb[listed(1, q + n, requests - 1)]
        q_copy(at, q).start()
        return carry

    lax.fori_loop(0, far, send_queries, 0)

    valid_0 = jnp.sum(jnp.where(lane == first_back, count, 0.0), axis=1, keepdims=True)
    valid_1 = jnp.sum(jnp.where(lane == second_back, count, 0.0), axis=1, keepdims=True)
    half = lane - jnp.where(lane >= float(2 * rows), float(2 * rows), 0.0)
    limits[0:n] = jnp.where(half < float(rows), valid_0, valid_1)

    place_lane = iota((n, HD), 1).astype(F32)

    def origins(number):
        mine = jnp.where(place_lane == place_0, 1.0, 0.0) + jnp.where(place_lane == place_1, 2.0, 0.0)
        return jnp.sum(jnp.where((mine > 0.0) & (number > 0.0), 2.0 * number - 2.0 + mine, 0.0), axis=0, keepdims=True)

    lists[0:1, 0:HD] = origins(near_number).astype(I32)
    lists[2:3, :] = origins(far_number).astype(I32)
    list_copy = pltpu.make_async_copy(lists, lists_s, list_sem)
    list_copy.start()
    list_copy.wait()

    for at in range(len(near_q)):
        near_copy(at).wait_recv()
    lane_1 = iota((1, HD), 1)
    own_lane = lane_1 // rows

    def stat_pair(logs, factors):
        low = lane_1 < 2 * rows
        return (
            jnp.where(low, logs, pltpu.roll(factors, 2 * rows, axis=1)),
            jnp.where(low, pltpu.roll(logs, 2 * rows, axis=1), factors),
        )

    def own_pages(step, carry):
        pair = (2 * step, 2 * step + 1)
        first_context, second_context = context_s[0, pair[0]], context_s[0, pair[1]]
        limit = jnp.where(own_lane < 2, first_context, second_context) - jnp.where(own_lane % 2 == 1, page, 0)
        keys, values = [], []
        for i in pair:
            for p in range(2):
                arrived = listed(0, p * requests + i, 2 * len(near_q))
                landed = jnp.maximum(arrived - 1, 0)
                at = table_s[p, i]
                keys.append(jnp.where(arrived > 0, near_in[landed, 0], kv[at]))
                values.append(jnp.where(arrived > 0, near_in[landed, 1], vv[at]))
        mine = [qb[i] for i in pair]
        maxima, totals, sums = column_sums(
            jnp.concatenate([mine[0], mine[0], mine[1], mine[1]], axis=0),
            keys, values, limit.astype(F32),
        )
        stats = stat_pair(maxima + jnp.log(totals), 1.0 / totals)
        for at, i in enumerate(pair):
            near[i] = sums[at * 2 * rows : (at + 1) * 2 * rows]
            near_stat[i] = stats[at]
        return carry

    lax.fori_loop(0, requests // 2, own_pages, 0, unroll=OWN)

    for i in range(requests):
        nk[i * steps : (i + 1) * steps, :] = nk_ref[i].astype(F32)
        nv[i * steps : (i + 1) * steps, :] = nv_ref[i].astype(F32)
    draft_keys = nk[...].astype(BF16)
    draft_values = nv[...].astype(BF16)
    chunk = HD // rows
    blocky = (HD, HD)
    key_at = iota(blocky, 1)
    row_at = iota(blocky, 0)

    def own_draft(c, carry):
        request = c * chunk + row_at // rows
        allowed = (key_at // steps == request) & (key_at % steps <= (row_at % rows) // heads)
        block = qb[pl.ds(c * chunk, chunk)].reshape(HD, HD)
        maxima, totals, sums = block_sums(block, draft_keys, draft_values, jnp.where(allowed, HUGE, MASKED))
        at = pl.ds(pl.multiple_of(c * HD, HD), HD)
        draft[at, :] = sums / totals
        draft_log[at, :] = jnp.broadcast_to(maxima + jnp.log(totals), blocky)
        return carry

    lax.fori_loop(0, requests // chunk, own_draft, 0, unroll=2)

    def sum_copy(at, q):
        return pltpu.make_async_remote_copy(
            src_ref=sum_out.at[pl.ds(2 * at, 2)], dst_ref=sum_in.at[pl.ds(2 * at, 2)], send_sem=sum_send, recv_sem=sum_recv,
            device_id=(ahead(q), lane_me), device_id_type=MESH,
        )

    def stat_copy(at, q):
        return pltpu.make_async_remote_copy(
            src_ref=stat_out.at[at], dst_ref=stat_in.at[at], send_sem=stat_send, recv_sem=stat_recv,
            device_id=(ahead(q), lane_me), device_id_type=MESH,
        )

    square_1 = iota(blocky, 0) == iota(blocky, 1)

    def serve_pair(start, pair):
        pages = [jnp.minimum(jnp.maximum(sources_s[0, q + k * n], 0), slots - 1) for q in pair for k in range(2)]
        ends = [limits[pl.ds(opposite(q), 1), :] for q in pair]
        maxima, totals, sums = column_sums(
            jnp.concatenate([q_in[start], q_in[start + 1]], axis=0),
            [kv[at] for at in pages], [vv[at] for at in pages], jnp.where(own_lane < 2, ends[0], ends[1]),
        )
        largest = jnp.maximum(jnp.max(jnp.abs(sums), axis=1, keepdims=True), 1e-30)
        coded = jnp.round(sums * (TOP / largest)).astype(I32).astype(jnp.int16)
        largest_row = jnp.sum(jnp.where(square_1, largest, 0.0), axis=0, keepdims=True)
        stats = stat_pair(maxima + jnp.log(totals), largest_row / (TOP * totals))
        for k in range(2):
            sum_out[pl.ds(2 * (start + k), 2)] = coded[k * 2 * rows : (k + 1) * 2 * rows].reshape(2, rows, HD)
            stat_out[start + k] = stats[k]

    def serve_some(start, qs):
        for at, q in enumerate(qs):
            q_copy(start + at, q).wait_recv()
        for at in range(0, len(qs), 2):
            serve_pair(start + at, (qs[at], qs[at + 1] if at + 1 < len(qs) else 0))
        for at, q in enumerate(qs):
            sum_copy(start + at, q).start()
            stat_copy(start + at, q).start()

    def serve(step, carry):
        serve_some(step * SERVE, [plan_s[step * SERVE + at] for at in range(SERVE)])
        return carry

    q_in[far] = jnp.zeros((2 * rows, HD), BF16)
    whole = (far - 1) // SERVE
    lax.fori_loop(0, whole, serve, 0)
    serve_some(whole * SERVE, far_q[whole * SERVE :])

    wait_all(sum_in, sum_recv, 0, 2 * far)
    wait_all(stat_in, stat_recv, 0, far)

    short = (rows, HD)
    skew = iota(short, 1) - iota(short, 0)

    def combine(i, carry):
        means, logs = [], []
        for p in range(2):
            origin = listed(2, p * requests + i, 2 * far)
            away = jnp.maximum(origin - 1, 0)
            moved = origin > 0
            stats = jnp.where(moved, stat_in[lax.div(away, 2)], near_stat[i])
            skip = jnp.where(moved, lax.rem(away, 2), p) * rows
            logs.append(jnp.sum(jnp.where(skew == skip, stats, 0.0), axis=1, keepdims=True))
            factor = jnp.sum(jnp.where(skew == skip + 2 * rows, stats, 0.0), axis=1, keepdims=True)
            means.append(jnp.where(moved, sum_in[away].astype(F32), near[i, pl.ds(p * rows, rows)]) * factor)
        at = pl.ds(pl.multiple_of(i * rows, rows), rows)
        means.append(draft[at, :])
        logs.append(draft_log[at, :])
        largest = jnp.maximum(jnp.maximum(logs[0], logs[1]), logs[2])
        factors = [jnp.exp(log - largest) for log in logs]
        numerator = factors[0] * means[0] + factors[1] * means[1] + factors[2] * means[2]
        result = numerator / (factors[0] + factors[1] + factors[2])
        attention[at, :] = result
        squares[i] = jnp.sum((result * result).reshape(steps, heads, HD), axis=1)
        return carry

    lax.fori_loop(0, requests, combine, 0, unroll=COMBINE)

    tokens = requests * steps
    total_c = jnp.sum(squares[...].reshape(tokens, HD), axis=1, keepdims=True)
    norm_rows[0] = to_row(total_c, tokens)

    def norm_copy(other):
        return pltpu.make_async_remote_copy(
            src_ref=norm_rows.at[0], dst_ref=norm_rows.at[other], send_sem=norm_send.at[other], recv_sem=norm_recv.at[other],
            device_id=(me, lax.rem(lane_me + other, tp)), device_id_type=MESH,
        )

    for other in range(1, tp):
        norm_copy(other).start()
    for other in range(1, tp):
        norm_copy(other).wait_recv()
    total = norm_rows[0]
    for other in range(1, tp):
        total = total + norm_rows[other]
    scale = lax.rsqrt(total * (1.0 / (tp * width)) + 1e-05)
    scales[...] = jnp.broadcast_to(to_column(scale, tokens), (tokens, HD)).reshape(requests, steps, HD)

    def finish(i, carry):
        for h in range(heads):
            at = slice(h * HD, (h + 1) * HD)
            out_ref[i, :, at] = attention[pl.ds(i * rows + h, steps, stride=heads), :] * scales[i] * gain_ref[:, at]
        return carry

    lax.fori_loop(0, requests, finish, 0)

    for other in range(1, tp):
        norm_copy(other).wait_send()
    for at in range(len(near_q)):
        near_copy(at).wait_send()
    wait_all(note_out, note_send, 1, n - 1)
    wait_all(q_out, q_send, 0, far)
    wait_all(sum_out, sum_send, 0, 2 * far)
    wait_all(stat_out, stat_send, 0, far)


def per_device(n, nz, tp, queries, new_keys, new_values, key_pool, value_pool, block_table, context, source, replica, target, gain):
    requests, steps, width = queries.shape
    rows = steps * width // HD
    slots, page, _ = key_pool.shape
    entries = source.shape[0]
    vmem = pl.BlockSpec(memory_space=pltpu.VMEM)
    anywhere = pl.BlockSpec(memory_space=pl.ANY)
    dma = pltpu.SemaphoreType.DMA
    table = block_table.T
    near, far = (len(distances) for distances in reach(n, nz))
    return pl.pallas_call(
        functools.partial(kernel, n, nz, tp),
        out_shape=jax.ShapeDtypeStruct((requests, steps, width), F32),
        in_specs=[anywhere] * 11,
        out_specs=vmem,
        scratch_shapes=[
            pltpu.SMEM((2, requests), I32),
            pltpu.SMEM((1, requests), I32),
            pltpu.VMEM((requests, steps, width), BF16),
            pltpu.VMEM((requests, steps, HD), BF16),
            pltpu.VMEM((requests, steps, HD), BF16),
            pltpu.VMEM((2, requests), I32),
            pltpu.VMEM((1, requests), I32),
            pltpu.VMEM((1, entries), I32),
            pltpu.VMEM((1, entries), I32),
            pltpu.VMEM((1, entries), I32),
            pltpu.VMEM((1, width), F32),
            pltpu.VMEM((slots, page, HD), BF16),
            pltpu.VMEM((slots, page, HD), BF16),
            pltpu.VMEM(((requests + 1) * rows, HD), F32),
            pltpu.VMEM((requests, rows, HD), BF16),
            pltpu.VMEM((requests * steps, HD), F32),
            pltpu.VMEM((requests * steps, HD), F32),
            pltpu.VMEM((2 * near, 2, page, HD), BF16),
            pltpu.VMEM((2 * near, 2, page, HD), BF16),
            pltpu.VMEM((n, 1, slots), I32),
            pltpu.VMEM((n, 1, slots), I32),
            pltpu.VMEM((8, HD), I32),
            pltpu.SMEM((8, HD), I32),
            pltpu.VMEM((8, HD), I32),
            pltpu.SMEM((8, HD), I32),
            pltpu.SMEM((far + 1,), I32),
            pltpu.VMEM((n + 8, slots), F32),
            pltpu.VMEM((far + 1, 2 * rows, HD), BF16),
            pltpu.VMEM((far + 1, 2 * rows, HD), BF16),
            pltpu.VMEM((2 * far + 2, rows, HD), jnp.int16),
            pltpu.VMEM((2 * far + 2, rows, HD), jnp.int16),
            pltpu.VMEM((far + 1, 1, HD), F32),
            pltpu.VMEM((far + 1, 1, HD), F32),
            pltpu.VMEM((requests, 2 * rows, HD), F32),
            pltpu.VMEM((requests, 1, HD), F32),
            pltpu.VMEM((requests * rows, HD), F32),
            pltpu.VMEM((requests * rows, HD), F32),
            pltpu.VMEM(((requests + 1) * rows, HD), F32),
            pltpu.VMEM((requests, steps, HD), F32),
            pltpu.VMEM((requests, steps, HD), F32),
            pltpu.VMEM((tp, 1, HD), F32),
            dma((13,)), dma, dma((near,)), dma((near,)), dma, dma, dma, dma((far,)), dma, dma, dma, dma, dma((tp,)), dma((tp,)),
        ],
        compiler_params=pltpu.CompilerParams(collective_id=0, has_side_effects=True, vmem_limit_bytes=56 * 2**20),
    )(
        queries, new_keys, new_values, key_pool, value_pool, table,
        context.reshape(1, requests), source.reshape(1, entries), replica.reshape(1, entries), target.reshape(1, entries),
        gain.reshape(1, width),
    )


def solution(mesh):
    n, tp = mesh.shape["rep"], mesh.shape["tp"]
    nz = 2 ** (n.bit_length() // 2)
    heads, replicas = P("rep", None, "tp"), P("rep")
    return jax.shard_map(
        functools.partial(per_device, n, nz, tp),
        mesh=mesh,
        in_specs=(heads, heads, heads, heads, heads, P("rep", None), replicas, replicas, replicas, replicas, P("tp")),
        out_specs=heads,
        check_vma=False,
    )
```

```python
import functools
import math

import jax
import jax.numpy as jnp
from jax import lax
from jax.experimental import pallas as pl
from jax.experimental.pallas import tpu as pltpu
from jax.sharding import PartitionSpec as P

HD = 128
MASKED = -1e30
HUGE = 3e38
TOP = 32767.0
OWN = 4
SERVE = 4
COMBINE = 8
STRIDE = 27
MESH = pl.DeviceIdType.MESH
I32 = jnp.int32
F32 = jnp.float32
BF16 = jnp.bfloat16


def iota(shape, dim):
    return lax.broadcasted_iota(I32, shape, dim)


def to_column(row, size):
    shape = (size, size)
    return jnp.sum(jnp.where(iota(shape, 0) == iota(shape, 1), row, 0.0), axis=1, keepdims=True)


def to_row(column, size):
    shape = (size, size)
    return jnp.sum(jnp.where(iota(shape, 0) == iota(shape, 1), column, 0.0), axis=0, keepdims=True)


def column_sums(queries, keys, values, limit):
    page = keys[0].shape[0]
    rows = HD // len(keys)
    shape = (page, HD)
    slot = iota(shape, 1) // rows
    products = [
        lax.dot_general(key, queries, (((1,), (1,)), ((), ())), preferred_element_type=F32) for key in keys
    ]
    scores = products[0]
    for b in range(1, len(keys)):
        scores = jnp.where(slot == b, products[b], scores)
    scores = jnp.where(iota(shape, 0).astype(F32) < limit, scores * (1.0 / math.sqrt(HD)), MASKED)
    maxima = jnp.max(scores, axis=0, keepdims=True)
    weights = jnp.exp(scores - maxima)
    totals = jnp.sum(weights, axis=0, keepdims=True)
    turned = weights.T.astype(BF16)
    sums = [
        jnp.dot(turned[b * rows : (b + 1) * rows], values[b], preferred_element_type=F32) for b in range(len(keys))
    ]
    return maxima, totals, jnp.concatenate(sums, axis=0)


def block_sums(queries, keys, values, caps):
    scores = lax.dot_general(queries, keys, (((1,), (1,)), ((), ())), preferred_element_type=F32)
    scores = jnp.minimum(scores * (1.0 / math.sqrt(HD)), caps)
    maxima = jnp.max(scores, axis=1, keepdims=True)
    weights = jnp.exp(scores - maxima)
    totals = jnp.sum(weights, axis=1, keepdims=True)
    sums = jnp.dot(weights.astype(BF16), values, preferred_element_type=F32)
    return maxima, totals, sums


def reach(n, nz):
    ny = n // nz
    near = [q for q in range(1, n) if hops(q, ny, nz) <= (2 if n > 16 else 1)]
    far, q = [], 0
    while len(far) < n - 1 - len(near):
        q = (q + STRIDE) % n
        if q and q not in near:
            far.append(q)
    return near, far


def hops(q, ny, nz):
    y, z = q // nz, q % nz
    return min(y, ny - y) + min(z, nz - z)


def kernel(
    n, nz, tp,
    q_hbm, nk_hbm, nv_hbm, kp_ref, vp_ref, table_hbm, context_hbm, source_hbm, replica_hbm, target_hbm, gain_hbm,
    out_ref,
    table_s, context_s, q_ref, nk_ref, nv_ref, table_ref, context_ref, source_ref, replica_ref, target_ref, gain_ref,
    kv, vv, qf, qb, nk, nv,
    near_out, near_in, note_out, note_in, lists, lists_s, sources, sources_s, plan_s, limits,
    q_out, q_in, sum_out, sum_in, stat_out, stat_in,
    near, near_stat, draft, draft_log, attention, laid, squares, scales, norm_rows,
    in_sem, list_sem, near_send, near_recv, note_send, note_recv, q_send, q_recv, sum_send, sum_recv, stat_send, stat_recv, norm_send, norm_recv,
):
    ny = n // nz
    requests, steps, width = q_hbm.shape
    heads = width // HD
    rows = steps * heads
    entries = replica_hbm.shape[1]
    slots = kp_ref.shape[0]
    page = kp_ref.shape[1]
    me = lax.axis_index("rep")
    lane_me = lax.axis_index("tp")
    my, mz = lax.div(me, nz), lax.rem(me, nz)

    def ahead(q):
        return lax.rem(my + lax.div(q, nz), ny) * nz + lax.rem(mz + lax.rem(q, nz), nz)

    def behind(q):
        return lax.rem(my + ny - lax.div(q, nz), ny) * nz + lax.rem(mz + nz - lax.rem(q, nz), nz)

    def opposite(q):
        return lax.rem(ny - lax.div(q, nz), ny) * nz + lax.rem(nz - lax.rem(q, nz), nz)

    def order(step):
        return lax.rem((step + 1) * STRIDE, n)

    near_q, far_q = reach(n, nz)
    far = len(far_q)

    moves = [
        (replica_hbm, replica_ref), (source_hbm, source_ref), (target_hbm, target_ref), (table_hbm, table_ref),
        (context_hbm, context_ref), (q_hbm, q_ref), (table_hbm, table_s), (context_hbm, context_s), (nk_hbm, nk_ref),
        (nv_hbm, nv_ref), (kp_ref, kv), (vp_ref, vv), (gain_hbm, gain_ref),
    ]
    fetches = [pltpu.make_async_copy(a, b, in_sem.at[at]) for at, (a, b) in enumerate(moves)]
    for fetch in fetches[0:5]:
        fetch.start()

    barrier = pltpu.get_barrier_semaphore()

    def greet(step, carry):
        pl.semaphore_signal(barrier, inc=1, device_id=(ahead(step + 1), lane_me), device_id_type=MESH)
        return carry

    lax.fori_loop(0, n - 1, greet, 0)
    for other in range(1, tp):
        pl.semaphore_signal(barrier, inc=1, device_id=(me, lax.rem(lane_me + other, tp)), device_id_type=MESH)

    for fetch in fetches[5:]:
        fetch.start()
    for at, q in enumerate(far_q):
        plan_s[at] = q
    for fetch in fetches[0:5]:
        fetch.wait()

    replica = replica_ref[...].astype(F32)
    source = source_ref[...].astype(F32)
    target = target_ref[...].astype(F32)
    square = (entries, entries)
    replica_c = to_column(replica, entries)
    same_before = (replica_c == replica) & (iota(square, 0) < iota(square, 1))
    rank = jnp.sum(jnp.where(same_before, 1.0, 0.0), axis=0, keepdims=True)
    rank_c = to_column(rank, entries)
    source_c = to_column(source, entries)

    def vector_peer(q, sign):
        dy, dz = q // nz, q % nz
        return (((my + ny + sign * dy) % ny) * nz + (mz + nz + sign * dz) % nz).astype(F32)

    def targets_of(sign):
        peers = vector_peer(iota((n, entries), 0), sign)
        found = []
        for k in range(2):
            chosen = (peers == replica) & (rank == float(k))
            found.append(jnp.sum(jnp.where(chosen, target + 1.0, 0.0), axis=1, keepdims=True) - 1.0)
        return found

    wide = (entries, 2 * n)
    peers_row = vector_peer(iota(wide, 1) % n, 1)
    chosen = (replica_c == peers_row) & (rank_c == (iota(wide, 1) // n).astype(F32))
    source_row = jnp.sum(jnp.where(chosen, source_c, 0.0), axis=0, keepdims=True)

    sources[...] = jnp.zeros(sources.shape, I32)
    sources[0:1, 0 : 2 * n] = source_row.astype(I32)
    source_copy = pltpu.make_async_copy(sources, sources_s, list_sem)
    source_copy.start()

    context_c = to_column(context_ref[...].astype(F32), requests)
    by_slot = (requests, slots)
    slot_lane = iota(by_slot, 1).astype(F32)
    request_c = iota(by_slot, 0).astype(F32)
    valid_row = jnp.zeros((1, slots), F32)
    place_row = jnp.zeros((1, slots), F32)
    for p in range(2):
        table_c = to_column(table_ref[p : p + 1, :].astype(F32), requests)
        here = table_c == slot_lane
        valid = jnp.clip(context_c - float(p * page), 0.0, float(page))
        valid_row += jnp.sum(jnp.where(here, valid, 0.0), axis=0, keepdims=True)
        place_row += jnp.sum(jnp.where(here, request_c + float(p * requests), 0.0), axis=0, keepdims=True)

    notes = (n, slots)
    lane = iota(notes, 1).astype(F32)
    first, second = targets_of(1)
    marks = jnp.where(lane == first, 65536.0, 0.0) + jnp.where(lane == second, 131072.0, 0.0)
    code = (valid_row + marks).astype(I32)
    for q in range(n):
        note_out[q] = code[q : q + 1, :]
    note_in[0] = jnp.zeros((1, slots), I32)
    pl.semaphore_wait(barrier, n - 1 + tp - 1)

    def note_copy(q):
        return pltpu.make_async_remote_copy(
            src_ref=note_out.at[q], dst_ref=note_in.at[q], send_sem=note_send, recv_sem=note_recv,
            device_id=(ahead(q), lane_me), device_id_type=MESH,
        )

    def send_note(step, carry):
        note_copy(order(step)).start()
        return carry

    lax.fori_loop(0, n - 1, send_note, 0)

    def near_copy(at):
        return pltpu.make_async_remote_copy(
            src_ref=near_out.at[pl.ds(2 * at, 2)], dst_ref=near_in.at[pl.ds(2 * at, 2)], send_sem=near_send.at[at],
            recv_sem=near_recv.at[at], device_id=(ahead(near_q[at]), lane_me), device_id_type=MESH,
        )

    for fetch in fetches[6:]:
        fetch.wait()
    source_copy.wait()
    for at, q in enumerate(near_q):
        for k in range(2):
            page_at = jnp.minimum(jnp.maximum(sources_s[0, q + k * n], 0), slots - 1)
            near_out[2 * at + k, 0] = kv[page_at]
            near_out[2 * at + k, 1] = vv[page_at]

    for at in range(len(near_q)):
        near_copy(at).start()
    first_back, second_back = targets_of(-1)
    q_at = iota((n, HD), 0)
    far_number = jnp.zeros((n, HD), F32)
    near_number = jnp.zeros((n, HD), F32)
    for at, q in enumerate(far_q):
        far_number = jnp.where(q_at == q, at + 1.0, far_number)
    for at, q in enumerate(near_q):
        near_number = jnp.where(q_at == q, at + 1.0, near_number)

    fetches[5].wait()

    def spread(i, carry):
        for h in range(heads):
            qf[pl.ds(i * rows + h, steps, stride=heads), :] = q_ref[i, :, h * HD : (h + 1) * HD].astype(F32)
        return carry

    lax.fori_loop(0, requests, spread, 0)

    def narrow(i, carry):
        qb[i] = qf[pl.ds(pl.multiple_of(i * rows, rows), rows), :].astype(BF16)
        return carry

    lax.fori_loop(0, requests, narrow, 0)

    def wait_all(buffer, sem, start, count):
        view = buffer.at[pl.ds(start, count)]
        pltpu.make_async_copy(view, view, sem).wait()

    wait_all(note_in, note_recv, 1, n - 1)

    got = note_in[...].reshape(n, slots)
    mark = got >> 16
    count = (got & 65535).astype(F32)
    place_0 = jnp.sum(jnp.where(mark == 1, place_row + 1.0, 0.0), axis=1, keepdims=True) - 1.0
    place_1 = jnp.sum(jnp.where(mark == 2, place_row + 1.0, 0.0), axis=1, keepdims=True) - 1.0
    line = (n, 2 * n)
    lane_2 = iota(line, 1)
    distance = iota(line, 0)
    request_0 = jnp.maximum(place_0, 0.0) - jnp.where(place_0 >= float(requests), float(requests), 0.0)
    request_1 = jnp.maximum(place_1, 0.0) - jnp.where(place_1 >= float(requests), float(requests), 0.0)
    request_row = jnp.sum(
        jnp.where(lane_2 == distance, request_0, 0.0) + jnp.where(lane_2 == distance + n, request_1, 0.0),
        axis=0, keepdims=True,
    )
    lists[...] = jnp.zeros(lists.shape, I32)
    lists[1:2, 0 : 2 * n] = request_row.astype(I32)
    list_copy = pltpu.make_async_copy(lists, lists_s, list_sem)
    list_copy.start()
    list_copy.wait()

    def listed(line, at, limit):
        return jnp.minimum(jnp.maximum(lists_s[line, at], 0), limit)

    def q_copy(at, q):
        return pltpu.make_async_remote_copy(
            src_ref=q_out.at[at], dst_ref=q_in.at[at], send_sem=q_send, recv_sem=q_recv.at[at],
            device_id=(behind(q), lane_me), device_id_type=MESH,
        )

    def send_queries(at, carry):
        q = plan_s[at]
        q_out[at, 0:rows] = qb[listed(1, q, requests - 1)]
        q_out[at, rows : 2 * rows] = qb[listed(1, q + n, requests - 1)]
        q_copy(at, q).start()
        return carry

    lax.fori_loop(0, far, send_queries, 0)

    valid_0 = jnp.sum(jnp.where(lane == first_back, count, 0.0), axis=1, keepdims=True)
    valid_1 = jnp.sum(jnp.where(lane == second_back, count, 0.0), axis=1, keepdims=True)
    half = lane - jnp.where(lane >= float(2 * rows), float(2 * rows), 0.0)
    limits[0:n] = jnp.where(half < float(rows), valid_0, valid_1)

    place_lane = iota((n, HD), 1).astype(F32)

    def origins(number):
        mine = jnp.where(place_lane == place_0, 1.0, 0.0) + jnp.where(place_lane == place_1, 2.0, 0.0)
        return jnp.sum(jnp.where((mine > 0.0) & (number > 0.0), 2.0 * number - 2.0 + mine, 0.0), axis=0, keepdims=True)

    lists[0:1, 0:HD] = origins(near_number).astype(I32)
    lists[2:3, :] = origins(far_number).astype(I32)
    list_copy = pltpu.make_async_copy(lists, lists_s, list_sem)
    list_copy.start()
    list_copy.wait()

    for at in range(len(near_q)):
        near_copy(at).wait_recv()
    lane_1 = iota((1, HD), 1)
    own_lane = lane_1 // rows

    def stat_pair(logs, factors):
        low = lane_1 < 2 * rows
        return (
            jnp.where(low, logs, pltpu.roll(factors, 2 * rows, axis=1)),
            jnp.where(low, pltpu.roll(logs, 2 * rows, axis=1), factors),
        )

    def own_pages(step, carry):
        pair = (2 * step, 2 * step + 1)
        first_context, second_context = context_s[0, pair[0]], context_s[0, pair[1]]
        limit = jnp.where(own_lane < 2, first_context, second_context) - jnp.where(own_lane % 2 == 1, page, 0)
        keys, values = [], []
        for i in pair:
            for p in range(2):
                arrived = listed(0, p * requests + i, 2 * len(near_q))
                landed = jnp.maximum(arrived - 1, 0)
                at = table_s[p, i]
                keys.append(jnp.where(arrived > 0, near_in[landed, 0], kv[at]))
                values.append(jnp.where(arrived > 0, near_in[landed, 1], vv[at]))
        mine = [qb[i] for i in pair]
        maxima, totals, sums = column_sums(
            jnp.concatenate([mine[0], mine[0], mine[1], mine[1]], axis=0),
            keys, values, limit.astype(F32),
        )
        stats = stat_pair(maxima + jnp.log(totals), 1.0 / totals)
        for at, i in enumerate(pair):
            near[i] = sums[at * 2 * rows : (at + 1) * 2 * rows]
            near_stat[i] = stats[at]
        return carry

    lax.fori_loop(0, requests // 2, own_pages, 0, unroll=OWN)

    for i in range(requests):
        nk[i * steps : (i + 1) * steps, :] = nk_ref[i].astype(F32)
        nv[i * steps : (i + 1) * steps, :] = nv_ref[i].astype(F32)
    draft_keys = nk[...].astype(BF16)
    draft_values = nv[...].astype(BF16)
    chunk = HD // rows
    blocky = (HD, HD)
    key_at = iota(blocky, 1)
    row_at = iota(blocky, 0)

    def own_draft(c, carry):
        request = c * chunk + row_at // rows
        allowed = (key_at // steps == request) & (key_at % steps <= (row_at % rows) // heads)
        block = qb[pl.ds(c * chunk, chunk)].reshape(HD, HD)
        maxima, totals, sums = block_sums(block, draft_keys, draft_values, jnp.where(allowed, HUGE, MASKED))
        at = pl.ds(pl.multiple_of(c * HD, HD), HD)
        draft[at, :] = sums / totals
        draft_log[at, :] = jnp.broadcast_to(maxima + jnp.log(totals), blocky)
        return carry

    lax.fori_loop(0, requests // chunk, own_draft, 0, unroll=2)

    def sum_copy(at, q):
        return pltpu.make_async_remote_copy(
            src_ref=sum_out.at[pl.ds(2 * at, 2)], dst_ref=sum_in.at[pl.ds(2 * at, 2)], send_sem=sum_send, recv_sem=sum_recv,
            device_id=(ahead(q), lane_me), device_id_type=MESH,
        )

    def stat_copy(at, q):
        return pltpu.make_async_remote_copy(
            src_ref=stat_out.at[at], dst_ref=stat_in.at[at], send_sem=stat_send, recv_sem=stat_recv,
            device_id=(ahead(q), lane_me), device_id_type=MESH,
        )

    square_1 = iota(blocky, 0) == iota(blocky, 1)

    def serve_pair(pair, qs):
        pages = [jnp.minimum(jnp.maximum(sources_s[0, q + k * n], 0), slots - 1) for q in qs for k in range(2)]
        ends = [limits[pl.ds(opposite(q), 1), :] for q in qs]
        maxima, totals, sums = column_sums(
            jnp.concatenate([q_in[at] for at in pair], axis=0),
            [kv[at] for at in pages], [vv[at] for at in pages], jnp.where(own_lane < 2, ends[0], ends[1]),
        )
        largest = jnp.maximum(jnp.max(jnp.abs(sums), axis=1, keepdims=True), 1e-30)
        coded = jnp.round(sums * (TOP / largest)).astype(I32).astype(jnp.int16)
        largest_row = jnp.sum(jnp.where(square_1, largest, 0.0), axis=0, keepdims=True)
        stats = stat_pair(maxima + jnp.log(totals), largest_row / (TOP * totals))
        for k, at in enumerate(pair):
            sum_out[pl.ds(2 * at, 2)] = coded[k * 2 * rows : (k + 1) * 2 * rows].reshape(2, rows, HD)
            stat_out[at] = stats[k]

    def serve_some(ats, qs):
        for at, q in zip(ats, qs):
            q_copy(at, q).wait_recv()
        for k in range(0, len(ats), 2):
            alone = k + 1 == len(ats)
            serve_pair((ats[k], far if alone else ats[k + 1]), (qs[k], 0 if alone else qs[k + 1]))
        for at, q in zip(ats, qs):
            sum_copy(at, q).start()
            stat_copy(at, q).start()

    def serve(step, carry):
        ats = [step * SERVE + turn for turn in range(SERVE)]
        serve_some(ats, [plan_s[at] for at in ats])
        return carry

    q_in[far] = jnp.zeros((2 * rows, HD), BF16)
    whole = (far - 1) // SERVE
    lax.fori_loop(0, whole, serve, 0)
    serve_some(list(range(whole * SERVE, far)), far_q[whole * SERVE :])

    wait_all(sum_in, sum_recv, 0, 2 * far)
    wait_all(stat_in, stat_recv, 0, far)

    short = (rows, HD)
    skew = iota(short, 1) - iota(short, 0)

    def combine(i, carry):
        means, logs = [], []
        for p in range(2):
            origin = listed(2, p * requests + i, 2 * far)
            away = jnp.maximum(origin - 1, 0)
            moved = origin > 0
            stats = jnp.where(moved, stat_in[lax.div(away, 2)], near_stat[i])
            skip = jnp.where(moved, lax.rem(away, 2), p) * rows
            logs.append(jnp.sum(jnp.where(skew == skip, stats, 0.0), axis=1, keepdims=True))
            factor = jnp.sum(jnp.where(skew == skip + 2 * rows, stats, 0.0), axis=1, keepdims=True)
            means.append(jnp.where(moved, sum_in[away].astype(F32), near[i, pl.ds(p * rows, rows)]) * factor)
        at = pl.ds(pl.multiple_of(i * rows, rows), rows)
        means.append(draft[at, :])
        logs.append(draft_log[at, :])
        largest = jnp.maximum(jnp.maximum(logs[0], logs[1]), logs[2])
        factors = [jnp.exp(log - largest) for log in logs]
        numerator = factors[0] * means[0] + factors[1] * means[1] + factors[2] * means[2]
        result = numerator / (factors[0] + factors[1] + factors[2])
        attention[at, :] = result
        squares[i] = jnp.sum((result * result).reshape(steps, heads, HD), axis=1)
        return carry

    lax.fori_loop(0, requests, combine, 0, unroll=COMBINE)

    tokens = requests * steps
    total_c = jnp.sum(squares[...].reshape(tokens, HD), axis=1, keepdims=True)
    norm_rows[0] = to_row(total_c, tokens)

    def norm_copy(other):
        return pltpu.make_async_remote_copy(
            src_ref=norm_rows.at[0], dst_ref=norm_rows.at[other], send_sem=norm_send.at[other], recv_sem=norm_recv.at[other],
            device_id=(me, lax.rem(lane_me + other, tp)), device_id_type=MESH,
        )

    for other in range(1, tp):
        norm_copy(other).start()

    def lay(i, carry):
        for h in range(heads):
            laid[i, :, h * HD : (h + 1) * HD] = attention[pl.ds(i * rows + h, steps, stride=heads), :]
        return carry

    lax.fori_loop(0, requests, lay, 0)

    for other in range(1, tp):
        norm_copy(other).wait_recv()
    total = norm_rows[0]
    for other in range(1, tp):
        total = total + norm_rows[other]
    scale = lax.rsqrt(total * (1.0 / (tp * width)) + 1e-05)
    scales[...] = jnp.broadcast_to(to_column(scale, tokens), (tokens, HD)).reshape(requests, steps, HD)

    def finish(i, carry):
        for h in range(heads):
            at = slice(h * HD, (h + 1) * HD)
            out_ref[i, :, at] = laid[i, :, at] * scales[i] * gain_ref[:, at]
        return carry

    lax.fori_loop(0, requests, finish, 0, unroll=4)

    for other in range(1, tp):
        norm_copy(other).wait_send()
    for at in range(len(near_q)):
        near_copy(at).wait_send()
    wait_all(note_out, note_send, 1, n - 1)
    wait_all(q_out, q_send, 0, far)
    wait_all(sum_out, sum_send, 0, 2 * far)
    wait_all(stat_out, stat_send, 0, far)


def per_device(n, nz, tp, queries, new_keys, new_values, key_pool, value_pool, block_table, context, source, replica, target, gain):
    requests, steps, width = queries.shape
    rows = steps * width // HD
    slots, page, _ = key_pool.shape
    entries = source.shape[0]
    vmem = pl.BlockSpec(memory_space=pltpu.VMEM)
    anywhere = pl.BlockSpec(memory_space=pltpu.HBM)
    dma = pltpu.SemaphoreType.DMA
    table = block_table.T
    near, far = (len(distances) for distances in reach(n, nz))
    return pl.pallas_call(
        functools.partial(kernel, n, nz, tp),
        out_shape=pltpu.VMEM((requests, steps, width), F32),
        in_specs=[anywhere] * 11,
        out_specs=vmem,
        scratch_shapes=[
            pltpu.SMEM((2, requests), I32),
            pltpu.SMEM((1, requests), I32),
            pltpu.VMEM((requests, steps, width), BF16),
            pltpu.VMEM((requests, steps, HD), BF16),
            pltpu.VMEM((requests, steps, HD), BF16),
            pltpu.VMEM((2, requests), I32),
            pltpu.VMEM((1, requests), I32),
            pltpu.VMEM((1, entries), I32),
            pltpu.VMEM((1, entries), I32),
            pltpu.VMEM((1, entries), I32),
            pltpu.VMEM((1, width), F32),
            pltpu.VMEM((slots, page, HD), BF16),
            pltpu.VMEM((slots, page, HD), BF16),
            pltpu.VMEM(((requests + 1) * rows, HD), F32),
            pltpu.VMEM((requests, rows, HD), BF16),
            pltpu.VMEM((requests * steps, HD), F32),
            pltpu.VMEM((requests * steps, HD), F32),
            pltpu.VMEM((2 * near, 2, page, HD), BF16),
            pltpu.VMEM((2 * near, 2, page, HD), BF16),
            pltpu.VMEM((n, 1, slots), I32),
            pltpu.VMEM((n, 1, slots), I32),
            pltpu.VMEM((8, HD), I32),
            pltpu.SMEM((8, HD), I32),
            pltpu.VMEM((8, HD), I32),
            pltpu.SMEM((8, HD), I32),
            pltpu.SMEM((far + 1,), I32),
            pltpu.VMEM((n + 8, slots), F32),
            pltpu.VMEM((far + 1, 2 * rows, HD), BF16),
            pltpu.VMEM((far + 1, 2 * rows, HD), BF16),
            pltpu.VMEM((2 * far + 2, rows, HD), jnp.int16),
            pltpu.VMEM((2 * far + 2, rows, HD), jnp.int16),
            pltpu.VMEM((far + 1, 1, HD), F32),
            pltpu.VMEM((far + 1, 1, HD), F32),
            pltpu.VMEM((requests, 2 * rows, HD), F32),
            pltpu.VMEM((requests, 1, HD), F32),
            pltpu.VMEM((requests * rows, HD), F32),
            pltpu.VMEM((requests * rows, HD), F32),
            pltpu.VMEM(((requests + 1) * rows, HD), F32),
            pltpu.VMEM((requests, steps, width), F32),
            pltpu.VMEM((requests, steps, HD), F32),
            pltpu.VMEM((requests, steps, HD), F32),
            pltpu.VMEM((tp, 1, HD), F32),
            dma((13,)), dma, dma((near,)), dma((near,)), dma, dma, dma, dma((far,)), dma, dma, dma, dma, dma((tp,)), dma((tp,)),
        ],
        compiler_params=pltpu.CompilerParams(collective_id=0, has_side_effects=True, vmem_limit_bytes=56 * 2**20),
    )(
        queries, new_keys, new_values, key_pool, value_pool, table,
        context.reshape(1, requests), source.reshape(1, entries), replica.reshape(1, entries), target.reshape(1, entries),
        gain.reshape(1, width),
    )


def solution(mesh):
    n, tp = mesh.shape["rep"], mesh.shape["tp"]
    nz = 2 ** (n.bit_length() // 2)
    heads, replicas = P("rep", None, "tp"), P("rep")
    return jax.shard_map(
        functools.partial(per_device, n, nz, tp),
        mesh=mesh,
        in_specs=(heads, heads, heads, heads, heads, P("rep", None), replicas, replicas, replicas, replicas, P("tp")),
        out_specs=heads,
        check_vma=False,
    )
```

```python
import functools
import math

import jax
import jax.numpy as jnp
from jax import lax
from jax.experimental import pallas as pl
from jax.experimental.pallas import tpu as pltpu
from jax.sharding import PartitionSpec as P

HD = 128
MASKED = -1e30
HUGE = 3e38
TOP = 32767.0
OWN = 4
SERVE = 4
COMBINE = 8
STRIDE = 27
MESH = pl.DeviceIdType.MESH
I32 = jnp.int32
F32 = jnp.float32
BF16 = jnp.bfloat16


def iota(shape, dim):
    return lax.broadcasted_iota(I32, shape, dim)


def to_column(row, size):
    shape = (size, size)
    return jnp.sum(jnp.where(iota(shape, 0) == iota(shape, 1), row, 0.0), axis=1, keepdims=True)


def to_row(column, size):
    shape = (size, size)
    return jnp.sum(jnp.where(iota(shape, 0) == iota(shape, 1), column, 0.0), axis=0, keepdims=True)


def column_sums(queries, keys, values, limit):
    page = keys[0].shape[0]
    rows = HD // len(keys)
    shape = (page, HD)
    slot = iota(shape, 1) // rows
    products = [
        lax.dot_general(key, queries, (((1,), (1,)), ((), ())), preferred_element_type=F32) for key in keys
    ]
    scores = products[0]
    for b in range(1, len(keys)):
        scores = jnp.where(slot == b, products[b], scores)
    scores = jnp.where(iota(shape, 0).astype(F32) < limit, scores * (1.0 / math.sqrt(HD)), MASKED)
    maxima = jnp.max(scores, axis=0, keepdims=True)
    weights = jnp.exp(scores - maxima)
    totals = jnp.sum(weights, axis=0, keepdims=True)
    turned = weights.T.astype(BF16)
    sums = [
        jnp.dot(turned[b * rows : (b + 1) * rows], values[b], preferred_element_type=F32) for b in range(len(keys))
    ]
    return maxima, totals, jnp.concatenate(sums, axis=0)


def block_sums(queries, keys, values, caps):
    scores = lax.dot_general(queries, keys, (((1,), (1,)), ((), ())), preferred_element_type=F32)
    scores = jnp.minimum(scores * (1.0 / math.sqrt(HD)), caps)
    maxima = jnp.max(scores, axis=1, keepdims=True)
    weights = jnp.exp(scores - maxima)
    totals = jnp.sum(weights, axis=1, keepdims=True)
    sums = jnp.dot(weights.astype(BF16), values, preferred_element_type=F32)
    return maxima, totals, sums


def reach(n, nz):
    ny = n // nz
    most = 2 if n > 16 else 1
    straight = [q for q in range(1, n) if q % nz == 0 or q // nz == 0]
    near = [q for q in range(1, n) if hops(q, ny, nz) <= most + (q in straight and n > 16)]
    far, q = [], 0
    while len(far) < n - 1 - len(near):
        q = (q + STRIDE) % n
        if q and q not in near:
            far.append(q)
    return near, far


def hops(q, ny, nz):
    y, z = q // nz, q % nz
    return min(y, ny - y) + min(z, nz - z)


def kernel(
    n, nz, tp,
    q_hbm, nk_hbm, nv_hbm, kp_ref, vp_ref, table_hbm, context_hbm, source_hbm, replica_hbm, target_hbm, gain_hbm,
    out_ref,
    table_s, context_s, q_ref, nk_ref, nv_ref, table_ref, context_ref, source_ref, replica_ref, target_ref, gain_ref,
    kv, vv, qf, qb, nk, nv,
    near_out, near_in, note_out, note_in, lists, lists_s, sources, sources_s, plan_s, limits,
    q_out, q_in, sum_out, sum_in, stat_out, stat_in,
    near, near_stat, draft, draft_log, attention, laid, squares, scales, norm_rows,
    in_sem, list_sem, near_send, near_recv, note_send, note_recv, q_send, q_recv, sum_send, sum_recv, stat_send, stat_recv, norm_send, norm_recv,
):
    ny = n // nz
    requests, steps, width = q_hbm.shape
    heads = width // HD
    rows = steps * heads
    entries = replica_hbm.shape[1]
    slots = kp_ref.shape[0]
    page = kp_ref.shape[1]
    me = lax.axis_index("rep")
    lane_me = lax.axis_index("tp")
    my, mz = lax.div(me, nz), lax.rem(me, nz)

    def ahead(q):
        return lax.rem(my + lax.div(q, nz), ny) * nz + lax.rem(mz + lax.rem(q, nz), nz)

    def behind(q):
        return lax.rem(my + ny - lax.div(q, nz), ny) * nz + lax.rem(mz + nz - lax.rem(q, nz), nz)

    def opposite(q):
        return lax.rem(ny - lax.div(q, nz), ny) * nz + lax.rem(nz - lax.rem(q, nz), nz)

    def order(step):
        return lax.rem((step + 1) * STRIDE, n)

    near_q, far_q = reach(n, nz)
    far = len(far_q)

    moves = [
        (replica_hbm, replica_ref), (source_hbm, source_ref), (target_hbm, target_ref), (table_hbm, table_ref),
        (context_hbm, context_ref), (q_hbm, q_ref), (table_hbm, table_s), (context_hbm, context_s), (nk_hbm, nk_ref),
        (nv_hbm, nv_ref), (kp_ref, kv), (vp_ref, vv), (gain_hbm, gain_ref),
    ]
    fetches = [pltpu.make_async_copy(a, b, in_sem.at[at]) for at, (a, b) in enumerate(moves)]
    for fetch in fetches[0:5]:
        fetch.start()

    barrier = pltpu.get_barrier_semaphore()

    def greet(step, carry):
        pl.semaphore_signal(barrier, inc=1, device_id=(ahead(step + 1), lane_me), device_id_type=MESH)
        return carry

    lax.fori_loop(0, n - 1, greet, 0)
    for other in range(1, tp):
        pl.semaphore_signal(barrier, inc=1, device_id=(me, lax.rem(lane_me + other, tp)), device_id_type=MESH)

    for fetch in fetches[5:]:
        fetch.start()
    for at, q in enumerate(far_q):
        plan_s[at] = q
    for fetch in fetches[0:5]:
        fetch.wait()

    replica = replica_ref[...].astype(F32)
    source = source_ref[...].astype(F32)
    target = target_ref[...].astype(F32)
    square = (entries, entries)
    replica_c = to_column(replica, entries)
    same_before = (replica_c == replica) & (iota(square, 0) < iota(square, 1))
    rank = jnp.sum(jnp.where(same_before, 1.0, 0.0), axis=0, keepdims=True)
    rank_c = to_column(rank, entries)
    source_c = to_column(source, entries)

    def vector_peer(q, sign):
        dy, dz = q // nz, q % nz
        return (((my + ny + sign * dy) % ny) * nz + (mz + nz + sign * dz) % nz).astype(F32)

    def targets_of(sign):
        peers = vector_peer(iota((n, entries), 0), sign)
        found = []
        for k in range(2):
            chosen = (peers == replica) & (rank == float(k))
            found.append(jnp.sum(jnp.where(chosen, target + 1.0, 0.0), axis=1, keepdims=True) - 1.0)
        return found

    wide = (entries, 2 * n)
    peers_row = vector_peer(iota(wide, 1) % n, 1)
    chosen = (replica_c == peers_row) & (rank_c == (iota(wide, 1) // n).astype(F32))
    source_row = jnp.sum(jnp.where(chosen, source_c, 0.0), axis=0, keepdims=True)

    sources[...] = jnp.zeros(sources.shape, I32)
    sources[0:1, 0 : 2 * n] = source_row.astype(I32)
    source_copy = pltpu.make_async_copy(sources, sources_s, list_sem)
    source_copy.start()

    context_c = to_column(context_ref[...].astype(F32), requests)
    by_slot = (requests, slots)
    slot_lane = iota(by_slot, 1).astype(F32)
    request_c = iota(by_slot, 0).astype(F32)
    valid_row = jnp.zeros((1, slots), F32)
    place_row = jnp.zeros((1, slots), F32)
    for p in range(2):
        table_c = to_column(table_ref[p : p + 1, :].astype(F32), requests)
        here = table_c == slot_lane
        valid = jnp.clip(context_c - float(p * page), 0.0, float(page))
        valid_row += jnp.sum(jnp.where(here, valid, 0.0), axis=0, keepdims=True)
        place_row += jnp.sum(jnp.where(here, request_c + float(p * requests), 0.0), axis=0, keepdims=True)

    notes = (n, slots)
    lane = iota(notes, 1).astype(F32)
    first, second = targets_of(1)
    marks = jnp.where(lane == first, 65536.0, 0.0) + jnp.where(lane == second, 131072.0, 0.0)
    code = (valid_row + marks).astype(I32)
    for q in range(n):
        note_out[q] = code[q : q + 1, :]
    note_in[0] = jnp.zeros((1, slots), I32)
    pl.semaphore_wait(barrier, n - 1 + tp - 1)

    def note_copy(q):
        return pltpu.make_async_remote_copy(
            src_ref=note_out.at[q], dst_ref=note_in.at[q], send_sem=note_send, recv_sem=note_recv,
            device_id=(ahead(q), lane_me), device_id_type=MESH,
        )

    def send_note(step, carry):
        note_copy(order(step)).start()
        return carry

    lax.fori_loop(0, n - 1, send_note, 0)

    def near_copy(at):
        return pltpu.make_async_remote_copy(
            src_ref=near_out.at[pl.ds(2 * at, 2)], dst_ref=near_in.at[pl.ds(2 * at, 2)], send_sem=near_send.at[at],
            recv_sem=near_recv.at[at], device_id=(ahead(near_q[at]), lane_me), device_id_type=MESH,
        )

    for fetch in fetches[6:]:
        fetch.wait()
    source_copy.wait()
    for at, q in enumerate(near_q):
        for k in range(2):
            page_at = jnp.minimum(jnp.maximum(sources_s[0, q + k * n], 0), slots - 1)
            near_out[2 * at + k, 0] = kv[page_at]
            near_out[2 * at + k, 1] = vv[page_at]

    for at in range(len(near_q)):
        near_copy(at).start()
    first_back, second_back = targets_of(-1)
    q_at = iota((n, HD), 0)
    far_number = jnp.zeros((n, HD), F32)
    near_number = jnp.zeros((n, HD), F32)
    for at, q in enumerate(far_q):
        far_number = jnp.where(q_at == q, at + 1.0, far_number)
    for at, q in enumerate(near_q):
        near_number = jnp.where(q_at == q, at + 1.0, near_number)

    fetches[5].wait()

    def spread(i, carry):
        for h in range(heads):
            qf[pl.ds(i * rows + h, steps, stride=heads), :] = q_ref[i, :, h * HD : (h + 1) * HD].astype(F32)
        return carry

    lax.fori_loop(0, requests, spread, 0)

    def narrow(i, carry):
        qb[i] = qf[pl.ds(pl.multiple_of(i * rows, rows), rows), :].astype(BF16)
        return carry

    lax.fori_loop(0, requests, narrow, 0)

    def wait_all(buffer, sem, start, count):
        view = buffer.at[pl.ds(start, count)]
        pltpu.make_async_copy(view, view, sem).wait()

    wait_all(note_in, note_recv, 1, n - 1)

    got = note_in[...].reshape(n, slots)
    mark = got >> 16
    count = (got & 65535).astype(F32)
    place_0 = jnp.sum(jnp.where(mark == 1, place_row + 1.0, 0.0), axis=1, keepdims=True) - 1.0
    place_1 = jnp.sum(jnp.where(mark == 2, place_row + 1.0, 0.0), axis=1, keepdims=True) - 1.0
    line = (n, 2 * n)
    lane_2 = iota(line, 1)
    distance = iota(line, 0)
    request_0 = jnp.maximum(place_0, 0.0) - jnp.where(place_0 >= float(requests), float(requests), 0.0)
    request_1 = jnp.maximum(place_1, 0.0) - jnp.where(place_1 >= float(requests), float(requests), 0.0)
    request_row = jnp.sum(
        jnp.where(lane_2 == distance, request_0, 0.0) + jnp.where(lane_2 == distance + n, request_1, 0.0),
        axis=0, keepdims=True,
    )
    lists[...] = jnp.zeros(lists.shape, I32)
    lists[1:2, 0 : 2 * n] = request_row.astype(I32)
    list_copy = pltpu.make_async_copy(lists, lists_s, list_sem)
    list_copy.start()
    list_copy.wait()

    def listed(line, at, limit):
        return jnp.minimum(jnp.maximum(lists_s[line, at], 0), limit)

    def q_copy(at, q):
        return pltpu.make_async_remote_copy(
            src_ref=q_out.at[at], dst_ref=q_in.at[at], send_sem=q_send, recv_sem=q_recv.at[at],
            device_id=(behind(q), lane_me), device_id_type=MESH,
        )

    def send_queries(at, carry):
        q = plan_s[at]
        q_out[at, 0:rows] = qb[listed(1, q, requests - 1)]
        q_out[at, rows : 2 * rows] = qb[listed(1, q + n, requests - 1)]
        q_copy(at, q).start()
        return carry

    lax.fori_loop(0, far, send_queries, 0)

    valid_0 = jnp.sum(jnp.where(lane == first_back, count, 0.0), axis=1, keepdims=True)
    valid_1 = jnp.sum(jnp.where(lane == second_back, count, 0.0), axis=1, keepdims=True)
    half = lane - jnp.where(lane >= float(2 * rows), float(2 * rows), 0.0)
    limits[0:n] = jnp.where(half < float(rows), valid_0, valid_1)

    place_lane = iota((n, HD), 1).astype(F32)

    def origins(number):
        mine = jnp.where(place_lane == place_0, 1.0, 0.0) + jnp.where(place_lane == place_1, 2.0, 0.0)
        return jnp.sum(jnp.where((mine > 0.0) & (number > 0.0), 2.0 * number - 2.0 + mine, 0.0), axis=0, keepdims=True)

    lists[0:1, 0:HD] = origins(near_number).astype(I32)
    lists[2:3, :] = origins(far_number).astype(I32)
    list_copy = pltpu.make_async_copy(lists, lists_s, list_sem)
    list_copy.start()
    list_copy.wait()

    for at in range(len(near_q)):
        near_copy(at).wait_recv()
    lane_1 = iota((1, HD), 1)
    own_lane = lane_1 // rows

    def stat_pair(logs, factors):
        low = lane_1 < 2 * rows
        return (
            jnp.where(low, logs, pltpu.roll(factors, 2 * rows, axis=1)),
            jnp.where(low, pltpu.roll(logs, 2 * rows, axis=1), factors),
        )

    def own_pages(step, carry):
        pair = (2 * step, 2 * step + 1)
        first_context, second_context = context_s[0, pair[0]], context_s[0, pair[1]]
        limit = jnp.where(own_lane < 2, first_context, second_context) - jnp.where(own_lane % 2 == 1, page, 0)
        keys, values = [], []
        for i in pair:
            for p in range(2):
                arrived = listed(0, p * requests + i, 2 * len(near_q))
                landed = jnp.maximum(arrived - 1, 0)
                at = table_s[p, i]
                keys.append(jnp.where(arrived > 0, near_in[landed, 0], kv[at]))
                values.append(jnp.where(arrived > 0, near_in[landed, 1], vv[at]))
        mine = [qb[i] for i in pair]
        maxima, totals, sums = column_sums(
            jnp.concatenate([mine[0], mine[0], mine[1], mine[1]], axis=0),
            keys, values, limit.astype(F32),
        )
        stats = stat_pair(maxima + jnp.log(totals), 1.0 / totals)
        for at, i in enumerate(pair):
            near[i] = sums[at * 2 * rows : (at + 1) * 2 * rows]
            near_stat[i] = stats[at]
        return carry

    lax.fori_loop(0, requests // 2, own_pages, 0, unroll=OWN)

    for i in range(requests):
        nk[i * steps : (i + 1) * steps, :] = nk_ref[i].astype(F32)
        nv[i * steps : (i + 1) * steps, :] = nv_ref[i].astype(F32)
    draft_keys = nk[...].astype(BF16)
    draft_values = nv[...].astype(BF16)
    chunk = HD // rows
    blocky = (HD, HD)
    key_at = iota(blocky, 1)
    row_at = iota(blocky, 0)

    def own_draft(c, carry):
        request = c * chunk + row_at // rows
        allowed = (key_at // steps == request) & (key_at % steps <= (row_at % rows) // heads)
        block = qb[pl.ds(c * chunk, chunk)].reshape(HD, HD)
        maxima, totals, sums = block_sums(block, draft_keys, draft_values, jnp.where(allowed, HUGE, MASKED))
        at = pl.ds(pl.multiple_of(c * HD, HD), HD)
        draft[at, :] = sums / totals
        draft_log[at, :] = jnp.broadcast_to(maxima + jnp.log(totals), blocky)
        return carry

    lax.fori_loop(0, requests // chunk, own_draft, 0, unroll=2)

    def sum_copy(at, q):
        return pltpu.make_async_remote_copy(
            src_ref=sum_out.at[pl.ds(2 * at, 2)], dst_ref=sum_in.at[pl.ds(2 * at, 2)], send_sem=sum_send, recv_sem=sum_recv,
            device_id=(ahead(q), lane_me), device_id_type=MESH,
        )

    def stat_copy(at, q):
        return pltpu.make_async_remote_copy(
            src_ref=stat_out.at[at], dst_ref=stat_in.at[at], send_sem=stat_send, recv_sem=stat_recv,
            device_id=(ahead(q), lane_me), device_id_type=MESH,
        )

    square_1 = iota(blocky, 0) == iota(blocky, 1)

    def serve_pair(pair, qs):
        pages = [jnp.minimum(jnp.maximum(sources_s[0, q + k * n], 0), slots - 1) for q in qs for k in range(2)]
        ends = [limits[pl.ds(opposite(q), 1), :] for q in qs]
        maxima, totals, sums = column_sums(
            jnp.concatenate([q_in[at] for at in pair], axis=0),
            [kv[at] for at in pages], [vv[at] for at in pages], jnp.where(own_lane < 2, ends[0], ends[1]),
        )
        largest = jnp.maximum(jnp.max(jnp.abs(sums), axis=1, keepdims=True), 1e-30)
        coded = jnp.round(sums * (TOP / largest)).astype(I32).astype(jnp.int16)
        largest_row = jnp.sum(jnp.where(square_1, largest, 0.0), axis=0, keepdims=True)
        stats = stat_pair(maxima + jnp.log(totals), largest_row / (TOP * totals))
        for k, at in enumerate(pair):
            sum_out[pl.ds(2 * at, 2)] = coded[k * 2 * rows : (k + 1) * 2 * rows].reshape(2, rows, HD)
            stat_out[at] = stats[k]

    def serve_some(ats, qs):
        for at, q in zip(ats, qs):
            q_copy(at, q).wait_recv()
        for k in range(0, len(ats), 2):
            alone = k + 1 == len(ats)
            serve_pair((ats[k], far if alone else ats[k + 1]), (qs[k], 0 if alone else qs[k + 1]))
        for at, q in zip(ats, qs):
            sum_copy(at, q).start()
            stat_copy(at, q).start()

    def serve(step, carry):
        ats = [step * SERVE + turn for turn in range(SERVE)]
        serve_some(ats, [plan_s[at] for at in ats])
        return carry

    q_in[far] = jnp.zeros((2 * rows, HD), BF16)
    whole = (far - 1) // SERVE
    lax.fori_loop(0, whole, serve, 0)
    serve_some(list(range(whole * SERVE, far)), far_q[whole * SERVE :])

    wait_all(sum_in, sum_recv, 0, 2 * far)
    wait_all(stat_in, stat_recv, 0, far)

    short = (rows, HD)
    skew = iota(short, 1) - iota(short, 0)

    def combine(i, carry):
        means, logs = [], []
        for p in range(2):
            origin = listed(2, p * requests + i, 2 * far)
            away = jnp.maximum(origin - 1, 0)
            moved = origin > 0
            stats = jnp.where(moved, stat_in[lax.div(away, 2)], near_stat[i])
            skip = jnp.where(moved, lax.rem(away, 2), p) * rows
            logs.append(jnp.sum(jnp.where(skew == skip, stats, 0.0), axis=1, keepdims=True))
            factor = jnp.sum(jnp.where(skew == skip + 2 * rows, stats, 0.0), axis=1, keepdims=True)
            means.append(jnp.where(moved, sum_in[away].astype(F32), near[i, pl.ds(p * rows, rows)]) * factor)
        at = pl.ds(pl.multiple_of(i * rows, rows), rows)
        means.append(draft[at, :])
        logs.append(draft_log[at, :])
        largest = jnp.maximum(jnp.maximum(logs[0], logs[1]), logs[2])
        factors = [jnp.exp(log - largest) for log in logs]
        numerator = factors[0] * means[0] + factors[1] * means[1] + factors[2] * means[2]
        result = numerator / (factors[0] + factors[1] + factors[2])
        attention[at, :] = result
        squares[i] = jnp.sum((result * result).reshape(steps, heads, HD), axis=1)
        return carry

    lax.fori_loop(0, requests, combine, 0, unroll=COMBINE)

    tokens = requests * steps
    total_c = jnp.sum(squares[...].reshape(tokens, HD), axis=1, keepdims=True)
    norm_rows[0] = to_row(total_c, tokens)

    def norm_copy(other):
        return pltpu.make_async_remote_copy(
            src_ref=norm_rows.at[0], dst_ref=norm_rows.at[other], send_sem=norm_send.at[other], recv_sem=norm_recv.at[other],
            device_id=(me, lax.rem(lane_me + other, tp)), device_id_type=MESH,
        )

    for other in range(1, tp):
        norm_copy(other).start()

    def lay(i, carry):
        for h in range(heads):
            laid[i, :, h * HD : (h + 1) * HD] = attention[pl.ds(i * rows + h, steps, stride=heads), :]
        return carry

    lax.fori_loop(0, requests, lay, 0)

    for other in range(1, tp):
        norm_copy(other).wait_recv()
    total = norm_rows[0]
    for other in range(1, tp):
        total = total + norm_rows[other]
    scale = lax.rsqrt(total * (1.0 / (tp * width)) + 1e-05)
    scales[...] = jnp.broadcast_to(to_column(scale, tokens), (tokens, HD)).reshape(requests, steps, HD)

    def finish(i, carry):
        for h in range(heads):
            at = slice(h * HD, (h + 1) * HD)
            out_ref[i, :, at] = laid[i, :, at] * scales[i] * gain_ref[:, at]
        return carry

    lax.fori_loop(0, requests, finish, 0, unroll=4)

    for other in range(1, tp):
        norm_copy(other).wait_send()
    for at in range(len(near_q)):
        near_copy(at).wait_send()
    wait_all(note_out, note_send, 1, n - 1)
    wait_all(q_out, q_send, 0, far)
    wait_all(sum_out, sum_send, 0, 2 * far)
    wait_all(stat_out, stat_send, 0, far)


def per_device(n, nz, tp, queries, new_keys, new_values, key_pool, value_pool, block_table, context, source, replica, target, gain):
    requests, steps, width = queries.shape
    rows = steps * width // HD
    slots, page, _ = key_pool.shape
    entries = source.shape[0]
    vmem = pl.BlockSpec(memory_space=pltpu.VMEM)
    anywhere = pl.BlockSpec(memory_space=pltpu.HBM)
    dma = pltpu.SemaphoreType.DMA
    table = block_table.T
    near, far = (len(distances) for distances in reach(n, nz))
    return pl.pallas_call(
        functools.partial(kernel, n, nz, tp),
        out_shape=pltpu.VMEM((requests, steps, width), F32),
        in_specs=[anywhere] * 11,
        out_specs=vmem,
        scratch_shapes=[
            pltpu.SMEM((2, requests), I32),
            pltpu.SMEM((1, requests), I32),
            pltpu.VMEM((requests, steps, width), BF16),
            pltpu.VMEM((requests, steps, HD), BF16),
            pltpu.VMEM((requests, steps, HD), BF16),
            pltpu.VMEM((2, requests), I32),
            pltpu.VMEM((1, requests), I32),
            pltpu.VMEM((1, entries), I32),
            pltpu.VMEM((1, entries), I32),
            pltpu.VMEM((1, entries), I32),
            pltpu.VMEM((1, width), F32),
            pltpu.VMEM((slots, page, HD), BF16),
            pltpu.VMEM((slots, page, HD), BF16),
            pltpu.VMEM(((requests + 1) * rows, HD), F32),
            pltpu.VMEM((requests, rows, HD), BF16),
            pltpu.VMEM((requests * steps, HD), F32),
            pltpu.VMEM((requests * steps, HD), F32),
            pltpu.VMEM((2 * near, 2, page, HD), BF16),
            pltpu.VMEM((2 * near, 2, page, HD), BF16),
            pltpu.VMEM((n, 1, slots), I32),
            pltpu.VMEM((n, 1, slots), I32),
            pltpu.VMEM((8, HD), I32),
            pltpu.SMEM((8, HD), I32),
            pltpu.VMEM((8, HD), I32),
            pltpu.SMEM((8, HD), I32),
            pltpu.SMEM((far + 1,), I32),
            pltpu.VMEM((n + 8, slots), F32),
            pltpu.VMEM((far + 1, 2 * rows, HD), BF16),
            pltpu.VMEM((far + 1, 2 * rows, HD), BF16),
            pltpu.VMEM((2 * far + 2, rows, HD), jnp.int16),
            pltpu.VMEM((2 * far + 2, rows, HD), jnp.int16),
            pltpu.VMEM((far + 1, 1, HD), F32),
            pltpu.VMEM((far + 1, 1, HD), F32),
            pltpu.VMEM((requests, 2 * rows, HD), F32),
            pltpu.VMEM((requests, 1, HD), F32),
            pltpu.VMEM((requests * rows, HD), F32),
            pltpu.VMEM((requests * rows, HD), F32),
            pltpu.VMEM(((requests + 1) * rows, HD), F32),
            pltpu.VMEM((requests, steps, width), F32),
            pltpu.VMEM((requests, steps, HD), F32),
            pltpu.VMEM((requests, steps, HD), F32),
            pltpu.VMEM((tp, 1, HD), F32),
            dma((13,)), dma, dma((near,)), dma((near,)), dma, dma, dma, dma((far,)), dma, dma, dma, dma, dma((tp,)), dma((tp,)),
        ],
        compiler_params=pltpu.CompilerParams(collective_id=0, has_side_effects=True, vmem_limit_bytes=56 * 2**20),
    )(
        queries, new_keys, new_values, key_pool, value_pool, table,
        context.reshape(1, requests), source.reshape(1, entries), replica.reshape(1, entries), target.reshape(1, entries),
        gain.reshape(1, width),
    )


def solution(mesh):
    n, tp = mesh.shape["rep"], mesh.shape["tp"]
    nz = 2 ** (n.bit_length() // 2)
    heads, replicas = P("rep", None, "tp"), P("rep")
    return jax.shard_map(
        functools.partial(per_device, n, nz, tp),
        mesh=mesh,
        in_specs=(heads, heads, heads, heads, heads, P("rep", None), replicas, replicas, replicas, replicas, P("tp")),
        out_specs=heads,
        check_vma=False,
    )
```
